128 devices in a mesh: row: 8 (over x, core), col: 16 (over z, y).
Axes of the slice: x: 4, y: 4, z: 4, core: 2. Of those that a mesh axis runs over, the one named last changes fastest.
Arguments:
- loaded: bfloat16 [1536, 8192], P('col', 'row'), may hold values from -6 to 6
- positions: int32 [1536], P('col'), may hold values from 0 to 1535, as said below
- gate_weight: bfloat16 [8192, 14336], P('row', 'col'), may hold values from -0.0625 to 0.0625
- up_weight: bfloat16 [8192, 14336], P('row', 'col'), may hold values from -0.0625 to 0.0625
- down_weight: bfloat16 [14336, 8192], P('col', 'row'), may hold values from -0.046875 to 0.046875
- segment: int32 [1536], P('col'), may hold values from 0 to 7, never falling along the last dimension, each value on 1 to 384 neighbouring positions
- log_ratio: float32 [1536], P('col'), may hold values from -6 to 6
- token_grad: bfloat16 [1536, 8192], P('col', 'row'), may hold values from -48 to 48
Outputs:
- mixed: bfloat16 [1536, 8192], P('col', 'row')
- grad_inputs: bfloat16 [1536, 8192], P('col', 'row')
- grad_gate: float32 [8192, 14336], P('row', 'col')
- grad_up: float32 [8192, 14336], P('row', 'col')
- grad_down: float32 [14336, 8192], P('col', 'row')
The draws below stay inside these ranges and needn't reach their ends.
Inputs may be any that keep to these rules, and one draw needn't show every extreme that they name: positions is a permutation of the 1536 packed positions. Loader block c holds loader rows c * 96 to (c + 1) * 96 - 1 and owner block b holds positions b * 96 to (b + 1) * 96 - 1; at most 18 rows of one loader block land in one owner block, and every draw reaches 18.
All inputs are finite; a program needn't handle non-finite values.
Results may differ from the reference program's by a relative error of at most 0.033.
Values may be sent and summed in bfloat16 or wider, within the bound.
A program may use at most 128 MiB of HBM per device.

```python
import math
import jax
import jax.numpy as jnp
import numpy as np
from jax import lax

D = 8192
FF = 14336
PAIRS = 4
TOKENS = 1536
ROWS_COL = 96
CAP = 18
SEG_MAX = 384
N_ROW = 8
N_COL = 16


def draw_positions(key, part):
    key = jax.random.fold_in(key, 11)
    key_shift, key_inner, key_outer = jax.random.split(key, 3)
    shifts = jax.random.permutation(key_shift, N_COL).astype(jnp.int32)
    inner = jax.vmap(lambda k: jax.random.permutation(k, ROWS_COL))(jax.random.split(key_inner, N_COL)).astype(jnp.int32)
    outer = jax.vmap(lambda k: jax.random.permutation(k, ROWS_COL))(jax.random.split(key_outer, N_COL)).astype(jnp.int32)
    source = jnp.arange(N_COL, dtype=jnp.int32)[:, None]
    which = inner // CAP
    owner = (source + shifts[which]) % N_COL
    place = outer[owner, inner]
    return (owner * ROWS_COL + place).reshape(-1).astype(jnp.int32)


def block_scale(key, dims, shards, smallest, high):
    loudness = 1.0
    for dim, parts in shards:
        steps = jax.random.uniform(jax.random.fold_in(jax.random.fold_in(key, 6), dim), (parts,), jnp.float32, smallest / len(shards), high / len(shards))
        loudness = loudness * jnp.repeat(jnp.exp(steps), dims[dim] // parts).reshape((-1,) + (1,) * (len(dims) - 1 - dim))
    return loudness


def length_profile(amount, total, limit, skew):
    portions = [(1 << 20) // math.isqrt(rank ** skew) + 1 for rank in range(2, amount + 1)]
    surplus, counts = total - limit - (amount - 1), [1] * (amount - 1)
    while surplus > 0:
        candidates = [i for i in range(amount - 1) if counts[i] < limit]
        pool, remaining = sum([portions[i] for i in candidates]), surplus
        for i in candidates:
            addition = min(limit - counts[i], max(1, remaining * portions[i] // pool), surplus)
            counts[i] = counts[i] + addition
            surplus = surplus - addition
    return np.array([limit] + counts)


def ragged_sizes(key, amount, total, limit, lean):
    if amount == 2:
        one = jax.random.randint(key, (), max(1, total - limit), min(limit, total - 1) + 1)
        return jnp.stack([one, total - one])
    lengths = jnp.asarray(length_profile(amount, total, limit, lean), jnp.int32)
    pairs = (amount - 1) // 2
    giver, taker = lengths[1:1 + 2 * pairs:2], lengths[2:2 + 2 * pairs:2]
    room = jnp.minimum(giver - 1, limit - taker)
    shifted = jax.random.randint(jax.random.fold_in(key, 1), (pairs,), 0, 1 << 20) % (room + 1)
    lengths = lengths.at[1:1 + 2 * pairs:2].set(giver - shifted).at[2:2 + 2 * pairs:2].set(taker + shifted)
    return lengths[jax.random.permutation(jax.random.fold_in(key, 2), amount)]


def scatter_about(rng, shape, scale, bound, cuts=(), kind=jnp.bfloat16):
    gain = block_scale(rng, shape, cuts, -0.22, 0.18) if cuts else 1.0
    result = jax.random.normal(rng, shape, jnp.float32) * scale * gain
    return jnp.minimum(jnp.maximum(result, -bound), bound).astype(kind)


def setup_inputs(seed: int = 0) -> dict:
    streams_of = jax.random.split(jax.random.key(seed), 9)
    loaded = scatter_about(streams_of[0], (TOKENS, D), 1.0, 6.0, ((0, 16), (1, 8)))
    positions = draw_positions(jax.random.fold_in(streams_of[8], 71), 0)
    gate_weight = scatter_about(streams_of[2], (D, FF), D ** -0.5, 0.0625, ((0, 8), (1, 16)))
    up_weight = scatter_about(streams_of[3], (D, FF), D ** -0.5, 0.0625, ((0, 8), (1, 16)))
    down_weight = scatter_about(streams_of[4], (FF, D), FF ** -0.5, 0.046875, ((0, 16), (1, 8)))
    segment = jnp.searchsorted(jnp.cumsum(ragged_sizes(streams_of[5], 2 * PAIRS, TOKENS, SEG_MAX, 1)), jnp.arange(TOKENS), side="right").astype(jnp.int32)
    log_ratio = scatter_about(streams_of[6], (TOKENS,), 0.5, 6.0, ((0, 16),), jnp.float32)
    token_grad = scatter_about(streams_of[7], (TOKENS, D), 8.0, 48.0, ((0, 16), (1, 8)))
    return {"loaded": loaded, "positions": positions, "gate_weight": gate_weight, "up_weight": up_weight, "down_weight": down_weight, "segment": segment, "log_ratio": log_ratio, "token_grad": token_grad}


BETA = 0.1


def block_sum(operand_pairs, pieces):
    total_rows = operand_pairs[0][0].shape[0]
    width_out = operand_pairs[0][1].shape[1]
    block_width = operand_pairs[0][0].shape[1] // pieces

    def advance(index, running):
        first_col = (index * block_width).astype(jnp.int32)
        partial_sum = jnp.zeros((total_rows, width_out), jnp.float32)
        for left_side, right_side in operand_pairs:
            left_part = lax.dynamic_slice_in_dim(left_side, first_col, block_width, 1)
            right_part = lax.dynamic_slice_in_dim(right_side, first_col, block_width, 0)
            partial_sum = partial_sum + jnp.dot(left_part, right_part, preferred_element_type=jnp.float32)
        rounded = lax.optimization_barrier(partial_sum.astype(jnp.bfloat16))
        return running + rounded.astype(jnp.float32)

    return lax.fori_loop(0, pieces, advance, jnp.zeros((total_rows, width_out), jnp.float32))


def reference(loaded, positions, gate_weight, up_weight, down_weight, segment, log_ratio, token_grad):
    inputs = jnp.zeros(loaded.shape, loaded.dtype).at[positions].set(loaded)
    gate_pre = block_sum([(inputs, gate_weight)], N_ROW)
    up_pre = block_sum([(inputs, up_weight)], N_ROW)
    hidden = (jax.nn.silu(gate_pre) * up_pre).astype(jnp.bfloat16)
    mixed = block_sum([(hidden, down_weight)], N_COL).astype(jnp.bfloat16)
    member = (segment[:, None] == jnp.arange(2 * PAIRS, dtype=jnp.int32)[None, :]).astype(jnp.float32)
    totals = jnp.sum(log_ratio[:, None] * member, 0)
    margin = BETA * (totals[0::2] - totals[1::2])
    pair_weight = -BETA * jax.nn.sigmoid(-margin)
    signed = jnp.stack([pair_weight, -pair_weight], 1).reshape(-1)
    token_weight = jnp.sum(member * signed[None, :], 1)
    out_grad = (token_weight[:, None] * token_grad.astype(jnp.float32)).astype(jnp.bfloat16)
    grad_hidden = block_sum([(out_grad, down_weight.T)], N_ROW)
    grad_down = jnp.dot(hidden.T, out_grad, preferred_element_type=jnp.float32)
    sigmoid_gate = jax.nn.sigmoid(gate_pre)
    act_gate = (grad_hidden * up_pre * sigmoid_gate * (1.0 + gate_pre * (1.0 - sigmoid_gate))).astype(jnp.bfloat16)
    act_up = (grad_hidden * gate_pre * sigmoid_gate).astype(jnp.bfloat16)
    grad_gate = jnp.dot(inputs.T, act_gate, preferred_element_type=jnp.float32)
    grad_up = jnp.dot(inputs.T, act_up, preferred_element_type=jnp.float32)
    grad_inputs = block_sum([(act_gate, gate_weight.T), (act_up, up_weight.T)], N_COL).astype(jnp.bfloat16)
    return (mixed, grad_inputs, grad_gate, grad_up, grad_down)
```

```python
import jax
import jax.numpy as jnp
from jax import lax
from jax.experimental import pallas as pl
from jax.experimental.pallas import tpu as pltpu
from jax.sharding import PartitionSpec as P

BETA = 0.1
F32, BF16 = jnp.float32, jnp.bfloat16
TOK, DB, FB = 1536, 1024, 896
BLOCK, HALF = 96, 48
CHUNK, SHARE = 384, 48
PLANE = 192
PLANE_OFF = (2, 1, -1, 0)
MINOR_OFF = (0, 1, -1, 2)
KINDS = dict(pre=2 * FB, gh=FB)
NT = (((0,), (0,)), ((), ()))
TN = (((1,), (1,)), ((), ()))


def rows(start, size):
    return pl.ds(start, size)


def kernel(info, loaded, token_grad, gw, uw, dw, mixed, ginp, ggate, gup, gdown, *scratch):
    (tiles, weights, down, xl, xs, grads, pre, pre_pair, pre_r1, pre_r2, pre_share, hid, ghp, gh_pair,
     gh_r1, gh_r2, act, part_m, part_i, c1, c2, c3, onehot, places, stage, stage_d, send, recv, local) = scratch
    row, col = lax.axis_index("row"), lax.axis_index("col")
    x, k, z, y = row // 2, row % 2, col // 4, col % 4

    def device(dx=0, dk=0, dz=0, dy=0):
        return {
            "row": lax.rem(x + dx + 4, 4) * 2 + lax.rem(k + dk, 2),
            "col": lax.rem(z + dz + 4, 4) * 4 + lax.rem(y + dy + 4, 4),
        }

    sent = []

    def transfer(src, dst, target, landing=None):
        index = len(sent)
        copy = pltpu.make_async_remote_copy(
            src_ref=src, dst_ref=dst, send_sem=send.at[index], recv_sem=recv.at[index],
            device_id=target, device_id_type=pl.DeviceIdType.MESH,
        )
        copy.start()
        sent.append(copy)
        if landing is None:
            return copy
        return pltpu.make_async_remote_copy(
            src_ref=src, dst_ref=landing, send_sem=send.at[index], recv_sem=recv.at[index],
            device_id=target, device_id_type=pl.DeviceIdType.MESH,
        )

    local_copies = []

    def fetch(src, dst):
        copy = pltpu.make_async_copy(src, dst, local.at[len(local_copies)])
        copy.start()
        local_copies.append(copy)
        return copy

    weight_copies = [fetch(gw, weights.at[:, 0:FB]), fetch(uw, weights.at[:, FB : 2 * FB]), fetch(dw, down)]

    others = [(dz, dy) for dz in range(4) for dy in range(4) if (dz, dy) != (0, 0)]
    barrier = pltpu.get_barrier_semaphore()
    peers = [device(dz=dz, dy=dy) for dz, dy in others]
    peers += [device(dx=1), device(dx=-1), device(dk=1)]
    for peer in peers:
        pl.semaphore_signal(barrier, inc=1, device_id=peer, device_id_type=pl.DeviceIdType.MESH)
    pl.semaphore_wait(barrier, len(peers))

    def along(half, major=0, minor=0):
        return device(dz=major, dy=minor) if half == 0 else device(dz=minor, dy=major)

    def place(half, plane, minor):
        return rows(half * 768 + plane * PLANE + minor * HALF, HALF)

    class Gather:
        def __init__(self, buf):
            self.buf, self.got = buf, {}

        def move(self, half, src, dst, target):
            self.got[(half,) + dst] = transfer(
                self.buf.at[place(half, *src)], self.buf.at[place(half, *dst)], target
            )

        def spread(self, half, minor):
            self.move(half, (3, minor), (2, minor), along(half, major=1))
            self.move(half, (3, minor), (1, minor), along(half, major=-1))

        def begin(self):
            for half in (0, 1):
                self.move(half, (3, 0), (3, 2), along(half, minor=1))
                self.move(half, (3, 0), (3, 1), along(half, minor=-1))
                self.move(half, (3, 0), (3, 3), along(half, minor=2))
                self.spread(half, 0)

        def wait(self, half, plane, minor):
            self.got[(half, plane, minor)].wait_recv()

        def first(self):
            for minor in (1, 2):
                for half in (0, 1):
                    self.wait(half, 3, minor)
                    self.spread(half, minor)
            for half in (0, 1):
                self.wait(half, 3, 3)
                self.spread(half, 3)

        def second(self):
            for half in (0, 1):
                self.wait(half, 2, 0)
                self.move(half, (2, 0), (0, 0), along(half, major=1))
            for half in (0, 1):
                self.wait(half, 2, 1)
                self.move(half, (2, 1), (0, 1), along(half, major=1))
            for half in (0, 1):
                self.wait(half, 1, 2)
                self.move(half, (1, 2), (0, 2), along(half, major=-1))
            for half in (0, 1):
                self.wait(half, 1, 3)
                self.move(half, (1, 3), (0, 3), along(half, major=-1))

        def finish(self):
            for half in (0, 1):
                for plane, minor in ((1, 0), (1, 1), (2, 2), (2, 3), (0, 0), (0, 1), (0, 2), (0, 3)):
                    self.wait(half, plane, minor)

    gather_x, gather_g = Gather(xl), Gather(grads)
    for half in (0, 1):
        xl[place(half, 3, 0), :] = loaded[rows(half * HALF, HALF), :]
    tiles[0:8, :] = info[...]
    gather_x.begin()
    tile_copies = []
    for dz, dy in others:
        slot = ((-dz) % 4) * 4 + (-dy) % 4
        tile_copies.append(
            transfer(tiles.at[0:8, :], tiles.at[slot * 8 : slot * 8 + 8, :], device(dz=dz, dy=dy))
        )
    gather_x.first()

    for copy in tile_copies:
        copy.wait_recv()
    table = tiles[...]
    turned = table.T

    def slot_of(half, plane, minor):
        major, less = PLANE_OFF[plane] % 4, MINOR_OFF[minor] % 4
        return major * 4 + less if half == 0 else less * 4 + major

    for half in (0, 1):
        for plane in range(4):
            for minor in range(4):
                lane = slot_of(half, plane, minor) * 8
                column = turned[half * HALF : half * HALF + HALF, lane : lane + 1]
                places[place(half, plane, minor), :] = jnp.broadcast_to(column, (HALF, 128)).astype(jnp.int32)
    kind = lax.broadcasted_iota(jnp.int32, (128, 128), 0) % 8
    segment_part = jnp.concatenate([table[8 * i + 1 : 8 * i + 2, :] for i in range(16)], 0)
    ratio_part = jnp.concatenate([table[8 * i + 2 : 8 * i + 3, :] for i in range(16)], 0)
    del kind

    def total(s):
        return jnp.sum(jnp.where(segment_part == float(s), ratio_part, 0.0), axis=(0, 1), keepdims=True)

    own_segment = turned[0:BLOCK, 1:2]
    token_weight = jnp.zeros((BLOCK, 1), F32)
    for p in range(4):
        margin = BETA * (total(2 * p) - total(2 * p + 1))
        pair_weight = -BETA * jax.nn.sigmoid(-margin)
        token_weight = jnp.where(own_segment == float(2 * p), pair_weight, token_weight)
        token_weight = jnp.where(own_segment == float(2 * p + 1), -pair_weight, token_weight)
    for half in (0, 1):
        part = rows(half * HALF, HALF)
        weight = token_weight[half * HALF : half * HALF + HALF, :]
        grads[place(half, 3, 0), :] = (weight * token_grad[part, :].astype(F32)).astype(BF16)
    gather_x.second()
    gather_x.finish()
    gather_g.begin()
    for copy in weight_copies:
        copy.wait()

    def permute(c):
        lane = lax.broadcasted_iota(jnp.int32, (1, CHUNK), 1)
        token = lane
        for j in range(8):
            half, plane, minor = c // 2, (c % 2) * 2 + j // 4, j % 4
            major, less = PLANE_OFF[plane], MINOR_OFF[minor]
            dz, dy = (major, less) if half == 0 else (less, major)
            block = lax.rem(z + dz + 4, 4) * 4 + lax.rem(y + dy + 4, 4)
            inside = (lane >= j * HALF) & (lane < (j + 1) * HALF)
            token = token + jnp.where(inside, block * BLOCK + half * HALF - j * HALF, 0)

        def build(i, carry):
            part = rows(pl.multiple_of(i * 128, 128), 128)
            match = places[part, 0:1] == token
            onehot[part, :] = jnp.where(match, 1.0, 0.0).astype(BF16)
            return carry

        lax.fori_loop(0, TOK // 128, build, 0)
        chunk = rows(c * CHUNK, CHUNK)
        xs[chunk, :] = lax.dot_general(onehot[...], xl[...], NT, preferred_element_type=F32).astype(BF16)

    def pre_matmul(c):
        chunk = rows(c * CHUNK, CHUNK)

        def tile(i, carry):
            cols = rows(pl.multiple_of(i * 256, 256), 256)
            pre[chunk, cols] = jnp.dot(xs[chunk, :], weights[:, cols], preferred_element_type=F32).astype(BF16)
            return carry

        lax.fori_loop(0, 7, tile, 0)

    def gh_matmul(c):
        chunk = rows(c * CHUNK, CHUNK)
        ghp[chunk, :] = lax.dot_general(grads[chunk, :], down[...], TN, preferred_element_type=F32).astype(BF16)

    def mixed_matmul(c):
        chunk = rows(c * CHUNK, CHUNK)

        def tile(i, carry):
            cols = rows(pl.multiple_of(i * 256, 256), 256)
            part_m[chunk, cols] = jnp.dot(hid[chunk, :], down[:, cols], preferred_element_type=F32).astype(BF16)
            return carry

        lax.fori_loop(0, 4, tile, 0)

    def ginp_matmul(c):
        chunk = rows(c * CHUNK, CHUNK)

        def tile(i, carry):
            cols = rows(pl.multiple_of(i * 256, 256), 256)
            part_i[chunk, cols] = lax.dot_general(
                act[chunk, :], weights[cols, :], TN, preferred_element_type=F32
            ).astype(BF16)
            return carry

        lax.fori_loop(0, 4, tile, 0)

    xp, xm, xo = lax.rem(x + 1, 4), lax.rem(x + 3, 4), lax.rem(x + 2, 4)

    class RowChunk:
        def __init__(self, c, part, pair, r1, r2, width, out, out_width):
            self.c, self.part, self.pair, self.r1, self.r2 = c, part, pair, r1, r2
            self.width, self.out, self.out_width = width, out, out_width

        def cut(self, width):
            if width == 2 * FB:
                return FB
            return 512 if self.c % 2 == 0 else 384

        def mine(self, xx):
            return rows(pl.multiple_of(self.c * CHUNK + k * PLANE + xx * SHARE, 16), SHARE)

        def pair_send(self):
            theirs = rows(pl.multiple_of(self.c * CHUNK + (1 - k) * PLANE, 16), PLANE)
            self.pair_copy = transfer(self.part.at[theirs, :], self.pair.at[self.c], device(dk=1))

        def pair_add(self):
            self.pair_copy.wait_recv()
            mine = rows(pl.multiple_of(self.c * CHUNK + k * PLANE, 16), PLANE)
            both = self.part[mine, :].astype(F32) + self.pair[self.c].astype(F32)
            self.part[mine, :] = both.astype(BF16)
            cut, far = self.cut(self.width), self.mine(xo)
            self.far = [
                transfer(self.part.at[far, 0:cut], self.r1.at[self.c, :, 0:cut], device(dx=1)),
                transfer(self.part.at[far, cut : self.width], self.r1.at[self.c, :, cut : self.width], device(dx=-1)),
            ]

        def ring_add(self):
            cut = self.cut(self.width)
            self.near = []
            for i, (xx, lo, hi, dx) in enumerate(((xp, 0, cut, 1), (xm, cut, self.width, -1))):
                self.far[i].wait_recv()
                mine = self.mine(xx)
                both = self.part[mine, lo:hi].astype(F32) + self.r1[self.c, :, lo:hi].astype(F32)
                self.part[mine, lo:hi] = both.astype(BF16)
                self.near.append(transfer(self.part.at[mine, :], self.r2.at[self.c, i], device(dx=dx)))

        def total(self):
            self.near[0].wait_recv()
            self.near[1].wait_recv()
            return (
                self.part[self.mine(x), :].astype(F32)
                + self.r2[self.c, 0].astype(F32)
                + self.r2[self.c, 1].astype(F32)
            )

        def out_send(self):
            own = self.out.at[self.mine(x), :]
            self.side = [
                transfer(own, own, device(dx=1), self.out.at[self.mine(xm), :]),
                transfer(own, own, device(dx=-1), self.out.at[self.mine(xp), :]),
            ]

        def out_forward(self):
            cut = self.cut(self.out_width)
            self.last = []
            for i, (xx, lo, hi, dx) in enumerate(((xm, 0, cut, 1), (xp, cut, self.out_width, -1))):
                self.side[i].wait_recv()
                piece = self.out.at[self.mine(xx), lo:hi]
                self.last.append(transfer(piece, piece, device(dx=dx), self.out.at[self.mine(xo), lo:hi]))

        def out_pair(self):
            self.last[0].wait_recv()
            self.last[1].wait_recv()
            mine = self.out.at[rows(pl.multiple_of(self.c * CHUNK + k * PLANE, 16), PLANE), :]
            theirs = self.out.at[rows(pl.multiple_of(self.c * CHUNK + (1 - k) * PLANE, 16), PLANE), :]
            self.done = transfer(mine, mine, device(dk=1), theirs)

        def out_wait(self):
            self.done.wait_recv()

    forward = [RowChunk(c, pre, pre_pair, pre_r1, pre_r2, 2 * FB, hid, FB) for c in range(4)]
    backward = [RowChunk(c, ghp, gh_pair, gh_r1, gh_r2, FB, act, 2 * FB) for c in range(4)]

    def hidden(c):
        both = forward[c].total()
        pre_share[c] = both
        gate, up = both[:, :FB], both[:, FB:]
        hid[forward[c].mine(x), :] = (gate * jax.nn.sigmoid(gate) * up).astype(BF16)
        forward[c].out_send()

    def acts(c):
        grad = backward[c].total()
        gate, up = pre_share[c, :, 0:FB], pre_share[c, :, FB : 2 * FB]
        s = jax.nn.sigmoid(gate)
        mine = backward[c].mine(x)
        act[mine, 0:FB] = (grad * up * s * (1.0 + gate * (1.0 - s))).astype(BF16)
        act[mine, FB : 2 * FB] = (grad * gate * s).astype(BF16)
        backward[c].out_send()

    class ColSum:
        def __init__(self, half, which, part, out):
            self.half, self.part, self.out = half, part, out
            self.c1, self.c2, self.c3 = c1.at[which], c2.at[which], c3.at[which]

        def plane(self, p):
            return self.half * 768 + p * PLANE

        def send_far(self):
            start = self.plane(0)
            self.far = [
                transfer(self.part.at[rows(start, 96), :], self.c1.at[0], along(self.half, major=1)),
                transfer(self.part.at[rows(start + 96, 96), :], self.c1.at[1], along(self.half, major=-1)),
            ]
            self.near = [None, None]

        def send_near(self, i):
            self.far[i].wait_recv()
            start = self.plane(1 + i)
            mine = rows(start + i * 96, 96)
            self.part[mine, :] = (self.part[mine, :].astype(F32) + self.c1[i].astype(F32)).astype(BF16)
            self.near[i] = transfer(
                self.part.at[rows(start, PLANE), :], self.c2.at[i], along(self.half, major=1 if i == 0 else -1)
            )

        def send_minor(self):
            self.near[0].wait_recv()
            self.near[1].wait_recv()
            own = rows(self.plane(3), PLANE)
            self.part[own, :] = (
                self.part[own, :].astype(F32) + self.c2[0].astype(F32) + self.c2[1].astype(F32)
            ).astype(BF16)
            self.minor = []
            for m in (1, 2, 3):
                self.minor.append(
                    transfer(
                        self.part.at[rows(self.plane(3) + m * HALF, HALF), :],
                        self.c3.at[m - 1],
                        along(self.half, minor=MINOR_OFF[m]),
                    )
                )

        def store(self):
            total = self.part[rows(self.plane(3), HALF), :].astype(F32)
            for i in range(3):
                self.minor[i].wait_recv()
                total = total + self.c3[i].astype(F32)
            self.out[rows(self.half * HALF, HALF), :] = total.astype(BF16)

    mixed_sum = [ColSum(h, h, part_m, mixed) for h in (0, 1)]
    ginp_sum = [ColSum(h, 2 + h, part_i, ginp) for h in (0, 1)]

    flush = {}

    def push(key, stage_ref, out_ref, value):
        if key in flush:
            flush[key].wait()
        stage_ref[...] = value
        flush[key] = fetch(stage_ref, out_ref)

    def down_grad(i):
        cols = rows(i * 256, 256)
        push(("d", i % 2), stage_d.at[i % 2], gdown.at[:, cols],
             lax.dot_general(hid[...], grads[:, cols], NT, preferred_element_type=F32))

    def up_grad(i):
        which, j = i // 4, i % 4
        cols = rows(j * 256, 256)
        target = (ggate, gup)[which]
        push(("u", i % 2), stage.at[i % 2], target.at[cols, :],
             lax.dot_general(xs[:, cols], act[:, which * FB : (which + 1) * FB], NT, preferred_element_type=F32))

    def step_pre(c):
        permute(c)
        pre_matmul(c)
        forward[c].pair_send()

    def step_gh(c):
        gh_matmul(c)
        backward[c].pair_send()

    step_pre(0)
    gather_g.first()
    step_pre(1)
    forward[0].pair_add()
    gather_g.second()
    step_pre(2)
    forward[0].ring_add()
    forward[1].pair_add()
    step_pre(3)
    hidden(0)
    forward[1].ring_add()
    forward[2].pair_add()
    gather_g.finish()
    step_gh(0)
    forward[0].out_forward()
    hidden(1)
    forward[2].ring_add()
    forward[3].pair_add()
    backward[0].pair_add()
    step_gh(1)
    forward[0].out_pair()
    forward[1].out_forward()
    hidden(2)
    forward[3].ring_add()
    backward[0].ring_add()
    backward[1].pair_add()
    step_gh(2)
    forward[0].out_wait()
    mixed_matmul(0)
    mixed_sum[0].send_far()
    forward[1].out_pair()
    forward[2].out_forward()
    hidden(3)
    acts(0)
    backward[1].ring_add()
    backward[2].pair_add()
    step_gh(3)
    forward[1].out_wait()
    mixed_matmul(1)
    mixed_sum[0].send_near(0)
    mixed_sum[0].send_near(1)
    forward[2].out_pair()
    forward[3].out_forward()
    backward[0].out_forward()
    acts(1)
    backward[2].ring_add()
    backward[3].pair_add()
    forward[2].out_wait()
    mixed_matmul(2)
    mixed_sum[1].send_far()
    forward[3].out_pair()
    backward[0].out_pair()
    backward[1].out_forward()
    acts(2)
    backward[3].ring_add()
    mixed_sum[0].send_minor()
    forward[3].out_wait()
    mixed_matmul(3)
    mixed_sum[1].send_near(0)
    mixed_sum[1].send_near(1)
    backward[0].out_wait()
    ginp_matmul(0)
    ginp_sum[0].send_far()
    backward[1].out_pair()
    backward[2].out_forward()
    acts(3)
    mixed_sum[0].store()
    down_grad(0)
    backward[1].out_wait()
    ginp_matmul(1)
    ginp_sum[0].send_near(0)
    ginp_sum[0].send_near(1)
    mixed_sum[1].send_minor()
    backward[2].out_pair()
    backward[3].out_forward()
    down_grad(1)
    backward[2].out_wait()
    ginp_matmul(2)
    ginp_sum[1].send_far()
    backward[3].out_pair()
    ginp_sum[0].send_minor()
    mixed_sum[1].store()
    down_grad(2)
    backward[3].out_wait()
    ginp_matmul(3)
    ginp_sum[1].send_near(0)
    ginp_sum[1].send_near(1)
    down_grad(3)
    for i in range(5):
        up_grad(i)
    ginp_sum[0].store()
    ginp_sum[1].send_minor()
    for i in range(5, 8):
        up_grad(i)
    ginp_sum[1].store()
    for copy in flush.values():
        copy.wait()
    for copy in sent:
        copy.wait_send()


def per_device(loaded, positions, gate_weight, up_weight, down_weight, segment, log_ratio, token_grad):
    info = jnp.stack([positions.astype(F32), segment.astype(F32), log_ratio], 0)
    info = jnp.pad(info, ((0, 5), (0, 128 - BLOCK)), constant_values=-1.0)
    vmem, anywhere = pl.BlockSpec(memory_space=pltpu.VMEM), pl.BlockSpec(memory_space=pl.ANY)
    shape = jax.ShapeDtypeStruct
    buf = lambda *s: pltpu.VMEM(s, BF16)
    transfers = 200
    scratch = [
        pltpu.VMEM((128, 128), F32),
        buf(DB, 2 * FB),
        buf(FB, DB),
        buf(TOK, DB),
        buf(TOK, DB),
        buf(TOK, DB),
        buf(TOK, 2 * FB),
        buf(4, PLANE, 2 * FB),
        buf(4, SHARE, 2 * FB),
        buf(4, 2, SHARE, 2 * FB),
        pltpu.VMEM((4, SHARE, 2 * FB), F32),
        buf(TOK, FB),
        buf(TOK, FB),
        buf(4, PLANE, FB),
        buf(4, SHARE, FB),
        buf(4, 2, SHARE, FB),
        buf(TOK, 2 * FB),
        buf(TOK, DB),
        buf(TOK, DB),
        buf(4, 2, 96, DB),
        buf(4, 2, PLANE, DB),
        buf(4, 3, HALF, DB),
        buf(TOK, CHUNK),
        pltpu.VMEM((TOK, 128), jnp.int32),
        pltpu.VMEM((2, 256, FB), F32),
        pltpu.VMEM((2, FB, 256), F32),
        pltpu.SemaphoreType.DMA((transfers,)),
        pltpu.SemaphoreType.DMA((transfers,)),
        pltpu.SemaphoreType.DMA((16,)),
    ]
    return pl.pallas_call(
        kernel,
        out_shape=(
            shape((BLOCK, DB), BF16),
            shape((BLOCK, DB), BF16),
            shape((DB, FB), F32),
            shape((DB, FB), F32),
            shape((FB, DB), F32),
        ),
        in_specs=[vmem] * 3 + [anywhere] * 3,
        out_specs=[vmem] * 2 + [anywhere] * 3,
        scratch_shapes=scratch,
        compiler_params=pltpu.CompilerParams(
            collective_id=0, has_side_effects=True, vmem_limit_bytes=64 * 1024 * 1024
        ),
        name="feed_forward",
    )(info, loaded, token_grad, gate_weight, up_weight, down_weight)


def solution(mesh):
    return jax.shard_map(
        per_device,
        mesh=mesh,
        in_specs=(
            P("col", "row"),
            P("col"),
            P("row", "col"),
            P("row", "col"),
            P("col", "row"),
            P("col"),
            P("col"),
            P("col", "row"),
        ),
        out_specs=(
            P("col", "row"),
            P("col", "row"),
            P("row", "col"),
            P("row", "col"),
            P("col", "row"),
        ),
        check_vma=False,
    )
```

```python
import jax
import jax.numpy as jnp
from jax import lax
from jax.experimental import pallas as pl
from jax.experimental.pallas import tpu as pltpu
from jax.sharding import PartitionSpec as P

BETA = 0.1
F32, BF16 = jnp.float32, jnp.bfloat16
TOK, DB, FB = 1536, 1024, 896
BLOCK, HALF = 96, 48
CHUNK, SHARE = 384, 48
PLANE = 192
FAR = 384
PLANE_OFF = (2, 1, -1, 0)
MINOR_OFF = (0, 1, -1, 2)
NT = (((0,), (0,)), ((), ()))
TN = (((1,), (1,)), ((), ()))


def rows(start, size):
    return pl.ds(start, size)


def kernel(spots, parts, ratios, loaded, token_grad, gw, uw, dw, mixed, ginp, ggate, gup, gdown, *scratch):
    (tiles, weights, down, xl, xs, grads, pre, pre_pair, pre_r1, pre_r2, pre_share, hid, ghp, gh_pair,
     gh_r1, gh_r2, act, part_m, c1, c2, c3, onehot, onehot_far, places, totals_u, totals_d, send, recv, local) = scratch
    part_i = xl
    row, col = lax.axis_index("row"), lax.axis_index("col")
    x, k, z, y = row // 2, row % 2, col // 4, col % 4

    def device(dx=0, dk=0, dz=0, dy=0):
        return {
            "row": lax.rem(x + dx + 4, 4) * 2 + lax.rem(k + dk, 2),
            "col": lax.rem(z + dz + 4, 4) * 4 + lax.rem(y + dy + 4, 4),
        }

    sent, gone = [], set()

    def transfer(src, dst, target, landing=None):
        index = len(sent)
        copy = pltpu.make_async_remote_copy(
            src_ref=src, dst_ref=dst, send_sem=send.at[index], recv_sem=recv.at[index],
            device_id=target, device_id_type=pl.DeviceIdType.MESH,
        )
        copy.start()
        sent.append(copy)
        if landing is None:
            return copy
        return pltpu.make_async_remote_copy(
            src_ref=src, dst_ref=landing, send_sem=send.at[index], recv_sem=recv.at[index],
            device_id=target, device_id_type=pl.DeviceIdType.MESH,
        )

    local_copies = []

    def fetch(src, dst):
        copy = pltpu.make_async_copy(src, dst, local.at[len(local_copies)])
        copy.start()
        local_copies.append(copy)
        return copy

    weight_copies = [fetch(gw, weights.at[:, 0:FB]), fetch(uw, weights.at[:, FB : 2 * FB]), fetch(dw, down)]

    others = [(dz, dy) for dz in range(4) for dy in range(4) if (dz, dy) != (0, 0)]
    barrier = pltpu.get_barrier_semaphore()
    peers = [device(dz=dz, dy=dy) for dz, dy in others]
    peers += [device(dx=1), device(dx=-1), device(dk=1)]
    for peer in peers:
        pl.semaphore_signal(barrier, inc=1, device_id=peer, device_id_type=pl.DeviceIdType.MESH)
    pl.semaphore_wait(barrier, len(peers))

    def along(half, major=0, minor=0):
        return device(dz=major, dy=minor) if half == 0 else device(dz=minor, dy=major)

    def place(half, plane, minor):
        return rows(plane * CHUNK + half * PLANE + minor * HALF, HALF)

    class Gather:
        def __init__(self, buf):
            self.buf, self.got, self.seen, self.left = buf, {}, set(), False

        def move(self, half, src, dst, target):
            self.got[(half,) + dst] = transfer(
                self.buf.at[place(half, *src)], self.buf.at[place(half, *dst)], target
            )

        def spread(self, half, minor):
            self.move(half, (3, minor), (2, minor), along(half, major=1))
            self.move(half, (3, minor), (1, minor), along(half, major=-1))

        def begin(self):
            for half in (0, 1):
                self.move(half, (3, 0), (3, 2), along(half, minor=1))
                self.move(half, (3, 0), (3, 1), along(half, minor=-1))
                self.move(half, (3, 0), (3, 3), along(half, minor=2))
                self.spread(half, 0)

        def wait(self, half, plane, minor):
            if (half, plane, minor) not in self.seen:
                self.got[(half, plane, minor)].wait_recv()
                self.seen.add((half, plane, minor))

        def spread_on(self, half, minor):
            self.wait(half, 3, minor)
            self.spread(half, minor)

        def forward(self, half, minor):
            plane, way = (2, 1) if minor < 2 else (1, -1)
            self.wait(half, plane, minor)
            self.move(half, (plane, minor), (0, minor), along(half, major=way))

        def need(self, *planes):
            for plane in planes:
                for half in (0, 1):
                    for minor in range(4):
                        if (plane, minor) != (3, 0):
                            self.wait(half, plane, minor)

    gather_x, gather_g = Gather(xl), Gather(grads)
    for half in (0, 1):
        xl[place(half, 3, 0), :] = loaded[rows(half * HALF, HALF), :]
    tiles[0:8, :] = jnp.full((8, 128), -1.0, F32)
    tiles[0:1, 0:BLOCK] = spots[...].astype(F32)
    tiles[1:2, 0:BLOCK] = parts[...].astype(F32)
    tiles[2:3, 0:BLOCK] = ratios[...]
    tile_copies = []

    def send_tiles():
        for dz, dy in others:
            slot = ((-dz) % 4) * 4 + (-dy) % 4
            tile_copies.append(
                transfer(tiles.at[0:8, :], tiles.at[slot * 8 : slot * 8 + 8, :], device(dz=dz, dy=dy))
            )

    def slot_of(half, plane, minor):
        major, less = PLANE_OFF[plane] % 4, MINOR_OFF[minor] % 4
        return major * 4 + less if half == 0 else less * 4 + major

    def tables():
        for copy in tile_copies:
            copy.wait_recv()
        table = tiles[...]
        turned = table.T
        for half in (0, 1):
            for plane in range(4):
                for minor in range(4):
                    lane = slot_of(half, plane, minor) * 8
                    column = turned[half * HALF : half * HALF + HALF, lane : lane + 1]
                    places[place(half, plane, minor), :] = jnp.broadcast_to(column, (HALF, 128)).astype(jnp.int32)
        segment_part = jnp.concatenate([table[8 * i + 1 : 8 * i + 2, :] for i in range(16)], 0)
        ratio_part = jnp.concatenate([table[8 * i + 2 : 8 * i + 3, :] for i in range(16)], 0)

        def total(s):
            return jnp.sum(jnp.where(segment_part == float(s), ratio_part, 0.0), axis=(0, 1), keepdims=True)

        own_segment = turned[0:BLOCK, 1:2]
        token_weight = jnp.zeros((BLOCK, 1), F32)
        for p in range(4):
            margin = BETA * (total(2 * p) - total(2 * p + 1))
            pair_weight = -BETA * jax.nn.sigmoid(-margin)
            token_weight = jnp.where(own_segment == float(2 * p), pair_weight, token_weight)
            token_weight = jnp.where(own_segment == float(2 * p + 1), -pair_weight, token_weight)
        for half in (0, 1):
            part = rows(half * HALF, HALF)
            weight = token_weight[half * HALF : half * HALF + HALF, :]
            grads[place(half, 3, 0), :] = (weight * token_grad[part, :].astype(F32)).astype(BF16)

    ready = []

    def need_weights():
        if not ready:
            for copy in weight_copies:
                copy.wait()
            ready.append(True)

    def tokens_of(c):
        lane = lax.broadcasted_iota(jnp.int32, (1, CHUNK), 1)
        token = lane
        for j in range(8):
            half, minor = j // 4, j % 4
            major, less = PLANE_OFF[c], MINOR_OFF[minor]
            dz, dy = (major, less) if half == 0 else (less, major)
            block = lax.rem(z + dz + 4, 4) * 4 + lax.rem(y + dy + 4, 4)
            inside = (lane >= j * HALF) & (lane < (j + 1) * HALF)
            token = token + jnp.where(inside, block * BLOCK + half * HALF - j * HALF, 0)
        return token

    def match(c, first, count, ref):
        token = tokens_of(c)

        def build(i, carry):
            part = rows(pl.multiple_of(i * 128, 128), 128)
            here = places[rows(pl.multiple_of(first + i * 128, 128), 128), 0:1]
            ref[part, :] = jnp.where(here == token, 1.0, 0.0).astype(BF16)
            return carry

        lax.fori_loop(0, count // 128, build, 0)

    def permute_most(c):
        gather_x.need(1, 2, 3)
        match(c, FAR, TOK - FAR, onehot)
        xs[rows(c * CHUNK, CHUNK), :] = lax.dot_general(
            onehot[...], xl[FAR:TOK, :], NT, preferred_element_type=F32
        ).astype(BF16)

    def permute_rest(c):
        gather_x.need(0)
        match(c, 0, FAR, onehot_far)
        chunk = rows(c * CHUNK, CHUNK)
        rest = lax.dot_general(onehot_far[...], xl[0:FAR, :], NT, preferred_element_type=F32)
        xs[chunk, :] = (xs[chunk, :].astype(F32) + rest).astype(BF16)

    def pre_matmul(c, i):
        need_weights()
        chunk, cols = rows(c * CHUNK, CHUNK), rows(i * FB, FB)
        pre[chunk, cols] = jnp.dot(xs[chunk, :], weights[:, cols], preferred_element_type=F32).astype(BF16)
        forward[c].pair_send(i)

    def gh_matmul(c):
        need_weights()
        gather_g.need(c)
        chunk = rows(c * CHUNK, CHUNK)
        ghp[chunk, :] = lax.dot_general(grads[chunk, :], down[...], TN, preferred_element_type=F32).astype(BF16)
        backward[c].pair_send(0)

    def mixed_matmul(c):
        chunk = rows(c * CHUNK, CHUNK)
        forward[c].out_wait()
        part_m[chunk, :] = jnp.dot(hid[chunk, :], down[...], preferred_element_type=F32).astype(BF16)

    def ginp_matmul(c):
        chunk = rows(c * CHUNK, CHUNK)
        backward[c].out_wait()
        if not gather_x.left:
            gather_x.left = True
            for copy in gather_x.got.values():
                copy.wait_send()
                gone.add(id(copy))
        part_i[chunk, :] = lax.dot_general(
            act[chunk, :], weights[...], TN, preferred_element_type=F32
        ).astype(BF16)

    xp, xm, xo = lax.rem(x + 1, 4), lax.rem(x + 3, 4), lax.rem(x + 2, 4)

    class RowChunk:
        def __init__(self, c, part, pair, r1, r2, width, out, out_width):
            self.c, self.part, self.pair, self.r1, self.r2 = c, part, pair, r1, r2
            self.width, self.out, self.out_width = width, out, out_width
            self.pairs, self.far, self.near, self.last = {}, {}, {}, {}

        def cut(self, width):
            if width == 2 * FB:
                return FB
            return 512 if self.c % 2 == 0 else 384

        def mine(self, xx):
            return rows(pl.multiple_of(self.c * CHUNK + k * PLANE + xx * SHARE, 16), SHARE)

        def pair_send(self, i):
            theirs = rows(pl.multiple_of(self.c * CHUNK + (1 - k) * PLANE, 16), PLANE)
            cols = rows(i * FB, FB)
            self.pairs[i] = transfer(self.part.at[theirs, cols], self.pair.at[self.c, :, cols], device(dk=1))

        def pair_add(self, i):
            self.pairs[i].wait_recv()
            mine, cols = rows(pl.multiple_of(self.c * CHUNK + k * PLANE, 16), PLANE), rows(i * FB, FB)
            both = self.part[mine, cols].astype(F32) + self.pair[self.c, :, cols].astype(F32)
            self.part[mine, cols] = both.astype(BF16)
            cut, far = self.cut(self.width), self.mine(xo)
            for way, lo, hi, dx in ((0, 0, cut, 1), (1, cut, self.width, -1)):
                if self.width == FB or way == i:
                    self.far[way] = transfer(
                        self.part.at[far, lo:hi], self.r1.at[self.c, :, lo:hi], device(dx=dx)
                    )

        def ring_add(self, i):
            cut = self.cut(self.width)
            xx, lo, hi, dx = ((xp, 0, cut, 1), (xm, cut, self.width, -1))[i]
            self.far[i].wait_recv()
            mine = self.mine(xx)
            both = self.part[mine, lo:hi].astype(F32) + self.r1[self.c, :, lo:hi].astype(F32)
            self.part[mine, lo:hi] = both.astype(BF16)
            self.near[i] = transfer(self.part.at[mine, :], self.r2.at[self.c, i], device(dx=dx))

        def total(self):
            self.near[0].wait_recv()
            self.near[1].wait_recv()
            return (
                self.part[self.mine(x), :].astype(F32)
                + self.r2[self.c, 0].astype(F32)
                + self.r2[self.c, 1].astype(F32)
            )

        def out_send(self):
            own = self.out.at[self.mine(x), :]
            self.side = [
                transfer(own, own, device(dx=1), self.out.at[self.mine(xm), :]),
                transfer(own, own, device(dx=-1), self.out.at[self.mine(xp), :]),
            ]

        def out_forward(self, i):
            cut = self.cut(self.out_width)
            xx, lo, hi, dx = ((xm, 0, cut, 1), (xp, cut, self.out_width, -1))[i]
            self.side[i].wait_recv()
            piece = self.out.at[self.mine(xx), lo:hi]
            self.last[i] = transfer(piece, piece, device(dx=dx), self.out.at[self.mine(xo), lo:hi])

        def out_pair(self):
            self.last[0].wait_recv()
            self.last[1].wait_recv()
            mine = self.out.at[rows(pl.multiple_of(self.c * CHUNK + k * PLANE, 16), PLANE), :]
            theirs = self.out.at[rows(pl.multiple_of(self.c * CHUNK + (1 - k) * PLANE, 16), PLANE), :]
            self.done = transfer(mine, mine, device(dk=1), theirs)

        def out_wait(self):
            if self.done is not None:
                self.done.wait_recv()
                self.done = None

    forward = [RowChunk(c, pre, pre_pair, pre_r1, pre_r2, 2 * FB, hid, FB) for c in range(4)]
    backward = [RowChunk(c, ghp, gh_pair, gh_r1, gh_r2, FB, act, 2 * FB) for c in range(4)]

    def hidden(c):
        both = forward[c].total()
        pre_share[c] = both
        gate, up = both[:, :FB], both[:, FB:]
        hid[forward[c].mine(x), :] = (gate * jax.nn.sigmoid(gate) * up).astype(BF16)
        forward[c].out_send()

    def acts(c):
        grad = backward[c].total()
        gate, up = pre_share[c, :, 0:FB], pre_share[c, :, FB : 2 * FB]
        s = jax.nn.sigmoid(gate)
        mine = backward[c].mine(x)
        act[mine, 0:FB] = (grad * up * s * (1.0 + gate * (1.0 - s))).astype(BF16)
        act[mine, FB : 2 * FB] = (grad * gate * s).astype(BF16)
        backward[c].out_send()

    class ColSum:
        def __init__(self, half, which, part, out):
            self.half, self.part, self.out = half, part, out
            self.c1, self.c2, self.c3 = c1.at[which], c2.at[which], c3.at[which]

        def plane(self, p):
            return p * CHUNK + self.half * PLANE

        def send_far(self):
            start = self.plane(0)
            self.far = [
                transfer(self.part.at[rows(start, 96), :], self.c1.at[0], along(self.half, major=1)),
                transfer(self.part.at[rows(start + 96, 96), :], self.c1.at[1], along(self.half, major=-1)),
            ]
            self.near = [None, None]

        def send_near(self, i):
            self.far[i].wait_recv()
            start = self.plane(1 + i)
            mine = rows(start + i * 96, 96)
            self.part[mine, :] = (self.part[mine, :].astype(F32) + self.c1[i].astype(F32)).astype(BF16)
            self.near[i] = transfer(
                self.part.at[rows(start, PLANE), :], self.c2.at[i], along(self.half, major=1 if i == 0 else -1)
            )

        def send_minor(self):
            self.near[0].wait_recv()
            self.near[1].wait_recv()
            own = rows(self.plane(3), PLANE)
            self.part[own, :] = (
                self.part[own, :].astype(F32) + self.c2[0].astype(F32) + self.c2[1].astype(F32)
            ).astype(BF16)
            self.minor = []
            for m in (1, 2, 3):
                self.minor.append(
                    transfer(
                        self.part.at[rows(self.plane(3) + m * HALF, HALF), :],
                        self.c3.at[m - 1],
                        along(self.half, minor=MINOR_OFF[m]),
                    )
                )

        def store(self):
            total = self.part[rows(self.plane(3), HALF), :].astype(F32)
            for i in range(3):
                self.minor[i].wait_recv()
                total = total + self.c3[i].astype(F32)
            self.out[rows(self.half * HALF, HALF), :] = total.astype(BF16)

    mixed_sum = [ColSum(h, h, part_m, mixed) for h in (0, 1)]
    ginp_sum = [ColSum(h, 2 + h, part_i, ginp) for h in (0, 1)]

    stores = []

    def down_grad(i):
        cols = rows(i * 256, 256)
        gather_g.need(0, 1, 2, 3)
        for c in range(4):
            forward[c].out_wait()
        totals_d[i] = lax.dot_general(hid[...], grads[:, cols], NT, preferred_element_type=F32)
        stores.append(fetch(totals_d.at[i], gdown.at[:, cols]))

    def up_grad(i, first, count):
        cols, part = rows(i % 4 * 256, 256), rows(first * CHUNK, count * CHUNK)
        wide = rows(i // 4 * FB, FB)
        for c in range(first, first + count):
            backward[c].out_wait()
        new = lax.dot_general(xs[part, cols], act[part, wide], NT, preferred_element_type=F32)
        totals_u[cols, wide] = totals_u[cols, wide] + new if first else new

    def up_grad_most(i):
        up_grad(i, 0, 3)

    def up_grad_rest(i):
        up_grad(i, 3, 1)
        cols = rows(i % 4 * 256, 256)
        stores.append(fetch(totals_u.at[cols, rows(i // 4 * FB, FB)], (ggate, gup)[i // 4].at[cols, :]))

    gather_x.begin()
    send_tiles()
    gather_x.forward(0, 0)
    gather_x.spread_on(0, 1)
    gather_x.spread_on(0, 2)
    gather_x.spread_on(1, 1)
    gather_x.spread_on(0, 3)
    gather_x.spread_on(1, 2)
    gather_x.forward(1, 0)
    gather_x.spread_on(1, 3)
    tables()
    gather_g.begin()
    gather_x.forward(1, 1)
    gather_x.forward(0, 1)
    gather_x.forward(0, 2)
    gather_x.forward(1, 2)
    gather_x.forward(0, 3)
    gather_x.forward(1, 3)
    gather_g.spread_on(0, 1)
    permute_most(2)
    permute_most(0)
    gather_g.spread_on(1, 1)
    gather_g.forward(0, 0)
    permute_most(1)
    gather_g.spread_on(1, 2)
    gather_g.spread_on(0, 3)
    gather_g.spread_on(0, 2)
    permute_most(3)
    gather_g.forward(1, 0)
    gather_g.spread_on(1, 3)
    gh_matmul(3)
    permute_rest(0)
    pre_matmul(0, 1)
    backward[3].pair_add(0)
    gather_g.forward(0, 1)
    pre_matmul(0, 0)
    forward[0].pair_add(1)
    gather_g.forward(1, 1)
    permute_rest(1)
    gather_g.forward(1, 2)
    gather_g.forward(0, 3)
    backward[3].ring_add(0)
    backward[3].ring_add(1)
    forward[0].pair_add(0)
    pre_matmul(1, 0)
    gather_g.forward(1, 3)
    gh_matmul(1)
    forward[0].ring_add(1)
    gather_g.forward(0, 2)
    forward[1].pair_add(0)
    pre_matmul(1, 1)
    backward[1].pair_add(0)
    permute_rest(3)
    forward[0].ring_add(0)
    permute_rest(2)
    forward[1].pair_add(1)
    gh_matmul(0)
    pre_matmul(2, 1)
    backward[1].ring_add(0)
    backward[1].ring_add(1)
    backward[0].pair_add(0)
    forward[1].ring_add(0)
    pre_matmul(2, 0)
    forward[2].pair_add(1)
    pre_matmul(3, 0)
    hidden(0)
    forward[2].pair_add(0)
    gh_matmul(2)
    forward[3].pair_add(0)
    backward[0].ring_add(1)
    backward[0].ring_add(0)
    forward[1].ring_add(1)
    pre_matmul(3, 1)
    backward[2].pair_add(0)
    forward[2].ring_add(1)
    forward[0].out_forward(1)
    forward[3].pair_add(1)
    forward[0].out_forward(0)
    forward[2].ring_add(0)
    hidden(1)
    forward[3].ring_add(0)
    acts(1)
    backward[2].ring_add(1)
    acts(0)
    backward[2].ring_add(0)
    forward[0].out_pair()
    mixed_matmul(0)
    mixed_sum[0].send_far()
    mixed_sum[1].send_far()
    hidden(2)
    forward[3].ring_add(1)
    forward[1].out_forward(1)
    forward[1].out_forward(0)
    backward[1].out_forward(1)
    backward[1].out_forward(0)
    backward[0].out_forward(1)
    forward[2].out_forward(1)
    backward[0].out_forward(0)
    acts(2)
    hidden(3)
    forward[2].out_forward(0)
    acts(3)
    forward[1].out_pair()
    mixed_matmul(1)
    mixed_sum[0].send_near(0)
    mixed_sum[1].send_near(0)
    backward[1].out_pair()
    backward[0].out_pair()
    ginp_matmul(1)
    ginp_matmul(0)
    forward[3].out_forward(0)
    ginp_sum[0].send_far()
    backward[2].out_forward(1)
    forward[3].out_forward(1)
    ginp_sum[1].send_far()
    backward[2].out_forward(0)
    forward[2].out_pair()
    mixed_matmul(2)
    mixed_sum[1].send_near(1)
    mixed_sum[0].send_near(1)
    backward[3].out_forward(1)
    backward[3].out_forward(0)
    forward[3].out_pair()
    backward[2].out_pair()
    ginp_sum[0].send_near(0)
    ginp_sum[1].send_near(0)
    down_grad(0)
    ginp_matmul(2)
    ginp_sum[0].send_near(1)
    ginp_sum[1].send_near(1)
    down_grad(1)
    down_grad(3)
    down_grad(2)
    mixed_matmul(3)
    mixed_sum[0].send_minor()
    mixed_sum[1].send_minor()
    backward[3].out_pair()
    up_grad_most(1)
    up_grad_most(5)
    up_grad_most(3)
    up_grad_rest(1)
    up_grad_rest(3)
    ginp_matmul(3)
    up_grad_rest(5)
    ginp_sum[0].send_minor()
    ginp_sum[1].send_minor()
    up_grad_most(6)
    up_grad_rest(6)
    up_grad_most(4)
    up_grad_rest(4)
    up_grad_most(2)
    up_grad_rest(2)
    mixed_sum[0].store()
    mixed_sum[1].store()
    up_grad_most(0)
    up_grad_rest(0)
    up_grad_most(7)
    up_grad_rest(7)
    ginp_sum[1].store()
    ginp_sum[0].store()
    for copy in stores:
        copy.wait()
    for copy in sent:
        if id(copy) not in gone:
            copy.wait_send()


COPIES = 26


def hand_over(*refs):
    sems = refs[10]
    copies = []
    for src, dst in zip(refs[:5], refs[5:10]):
        pieces = 8 if src.dtype == F32 else 1
        size = src.shape[0] // pieces
        for i in range(pieces):
            part = rows(i * size, size)
            copies.append(pltpu.make_async_copy(src.at[part, :], dst.at[part, :], sems.at[len(copies)]))
    for copy in copies:
        copy.start()
    for copy in copies:
        copy.wait()


def per_device(loaded, positions, gate_weight, up_weight, down_weight, segment, log_ratio, token_grad):
    vmem, anywhere = pl.BlockSpec(memory_space=pltpu.VMEM), pl.BlockSpec(memory_space=pl.ANY)
    shape = jax.ShapeDtypeStruct
    buf = lambda *s: pltpu.VMEM(s, BF16)
    transfers = 200
    scratch = [
        pltpu.VMEM((128, 128), F32),
        buf(DB, 2 * FB),
        buf(FB, DB),
        buf(TOK, DB),
        buf(TOK, DB),
        buf(TOK, DB),
        buf(TOK, 2 * FB),
        buf(4, PLANE, 2 * FB),
        buf(4, SHARE, 2 * FB),
        buf(4, 2, SHARE, 2 * FB),
        pltpu.VMEM((4, SHARE, 2 * FB), F32),
        buf(TOK, FB),
        buf(TOK, FB),
        buf(4, PLANE, FB),
        buf(4, SHARE, FB),
        buf(4, 2, SHARE, FB),
        buf(TOK, 2 * FB),
        buf(TOK, DB),
        buf(4, 2, 96, DB),
        buf(4, 2, PLANE, DB),
        buf(4, 3, HALF, DB),
        buf(TOK - FAR, CHUNK),
        buf(FAR, CHUNK),
        pltpu.VMEM((TOK, 128), jnp.int32),
        pltpu.VMEM((DB, 2 * FB), F32),
        pltpu.VMEM((4, FB, 256), F32),
        pltpu.SemaphoreType.DMA((transfers,)),
        pltpu.SemaphoreType.DMA((transfers,)),
        pltpu.SemaphoreType.DMA((16,)),
    ]
    outs = pl.pallas_call(
        kernel,
        out_shape=(
            shape((BLOCK, DB), BF16),
            shape((BLOCK, DB), BF16),
            shape((DB, FB), F32),
            shape((DB, FB), F32),
            shape((FB, DB), F32),
        ),
        in_specs=[vmem] * 5 + [anywhere] * 3,
        out_specs=[vmem] * 2 + [anywhere] * 3,
        scratch_shapes=scratch,
        compiler_params=pltpu.CompilerParams(
            collective_id=0, has_side_effects=True, vmem_limit_bytes=64 * 1024 * 1024
        ),
        name="feed_forward",
    )(
        positions.reshape(1, BLOCK), segment.reshape(1, BLOCK), log_ratio.reshape(1, BLOCK),
        loaded, token_grad, gate_weight, up_weight, down_weight,
    )
    return pl.pallas_call(
        hand_over,
        out_shape=tuple(shape(o.shape, o.dtype) for o in outs),
        in_specs=[anywhere] * 5,
        out_specs=[anywhere] * 5,
        scratch_shapes=[pltpu.SemaphoreType.DMA((COPIES,))],
        name="hand_over",
    )(*outs)


def solution(mesh):
    return jax.shard_map(
        per_device,
        mesh=mesh,
        in_specs=(
            P("col", "row"),
            P("col"),
            P("row", "col"),
            P("row", "col"),
            P("col", "row"),
            P("col"),
            P("col"),
            P("col", "row"),
        ),
        out_specs=(
            P("col", "row"),
            P("col", "row"),
            P("row", "col"),
            P("row", "col"),
            P("col", "row"),
        ),
        check_vma=False,
    )
```

```python
import jax
import jax.numpy as jnp
from jax import lax
from jax.experimental import pallas as pl
from jax.experimental.pallas import tpu as pltpu
from jax.sharding import PartitionSpec as P

BETA = 0.1
F32, BF16 = jnp.float32, jnp.bfloat16
TOK, DB, FB = 1536, 1024, 896
BLOCK, HALF = 96, 48
CHUNK, SHARE = 384, 48
PLANE = 192
FAR = 384
PLANE_OFF = (2, 1, -1, 0)
MINOR_OFF = (0, 1, -1, 2)
CHUNKS = (
    ((0, 0), (0, 1), (0, 2), (0, 3)),
    ((1, 0), (1, 1), (2, 2), (2, 3)),
    ((2, 0), (2, 1), (1, 2), (1, 3)),
    ((3, 0), (3, 1), (3, 2), (3, 3)),
)
NT = (((0,), (0,)), ((), ()))
TN = (((1,), (1,)), ((), ()))


def rows(start, size):
    return pl.ds(start, size)


def kernel(spots, parts, ratios, loaded, token_grad, gw, uw, dw, mixed, ginp, ggate, gup, gdown, *scratch):
    (tiles, weights, down, xl, xs, grads, pre, pre_pair, pre_r1, pre_r2, pre_share, hid, ghp, gh_pair,
     gh_r1, gh_r2, act, part_m, c1, c2, c3, onehot, onehot_far, places, totals_u, totals_d, small_u, small_s, small_f, held_grad, send, recv, local) = scratch
    part_i = xl
    row, col = lax.axis_index("row"), lax.axis_index("col")
    x, k, z, y = row // 2, row % 2, col // 4, col % 4

    def device(dx=0, dk=0, dz=0, dy=0):
        return {
            "row": lax.rem(x + dx + 4, 4) * 2 + lax.rem(k + dk, 2),
            "col": lax.rem(z + dz + 4, 4) * 4 + lax.rem(y + dy + 4, 4),
        }

    sent, gone = [], set()

    def transfer(src, dst, target, landing=None):
        index = len(sent)
        copy = pltpu.make_async_remote_copy(
            src_ref=src, dst_ref=dst, send_sem=send.at[index], recv_sem=recv.at[index],
            device_id=target, device_id_type=pl.DeviceIdType.MESH,
        )
        copy.start()
        sent.append(copy)
        if landing is None:
            return copy
        return pltpu.make_async_remote_copy(
            src_ref=src, dst_ref=landing, send_sem=send.at[index], recv_sem=recv.at[index],
            device_id=target, device_id_type=pl.DeviceIdType.MESH,
        )

    local_copies = []

    def fetch(src, dst):
        copy = pltpu.make_async_copy(src, dst, local.at[len(local_copies)])
        copy.start()
        local_copies.append(copy)
        return copy

    def along(half, major=0, minor=0):
        return device(dz=major, dy=minor) if half == 0 else device(dz=minor, dy=major)

    def place(half, plane, minor):
        for c, held in enumerate(CHUNKS):
            if (plane, minor) in held:
                return rows(c * CHUNK + half * PLANE + held.index((plane, minor)) * HALF, HALF)

    sources = (spots, parts, ratios, token_grad)
    spots, parts, ratios, token_grad = small_u, small_s, small_f, held_grad
    first_copies = [
        fetch(loaded.at[rows(half * HALF, HALF), :], xl.at[place(half, 3, 0), :]) for half in (0, 1)
    ]
    small_copies = [fetch(a, b) for a, b in zip(sources, (spots, parts, ratios, token_grad))]
    weight_copies = [fetch(gw, weights.at[:, 0:FB]), fetch(uw, weights.at[:, FB : 2 * FB]), fetch(dw, down)]

    others = [(dz, dy) for dz in range(4) for dy in range(4) if (dz, dy) != (0, 0)]
    barrier = pltpu.get_barrier_semaphore()
    peers = [device(dz=dz, dy=dy) for dz, dy in others]
    peers += [device(dx=1), device(dx=-1), device(dk=1)]
    for peer in peers:
        pl.semaphore_signal(barrier, inc=1, device_id=peer, device_id_type=pl.DeviceIdType.MESH)
    pl.semaphore_wait(barrier, len(peers))

    class Gather:
        def __init__(self, buf):
            self.buf, self.got, self.seen, self.left = buf, {}, set(), False

        def move(self, half, src, dst, target):
            self.got[(half,) + dst] = transfer(
                self.buf.at[place(half, *src)], self.buf.at[place(half, *dst)], target
            )

        def spread(self, half, minor):
            self.move(half, (3, minor), (2, minor), along(half, major=1))
            self.move(half, (3, minor), (1, minor), along(half, major=-1))

        def begin(self):
            for half in (0, 1):
                self.move(half, (3, 0), (3, 2), along(half, minor=1))
                self.move(half, (3, 0), (3, 1), along(half, minor=-1))
                self.move(half, (3, 0), (3, 3), along(half, minor=2))
                self.spread(half, 0)

        def wait(self, half, plane, minor):
            if (half, plane, minor) not in self.seen:
                self.got[(half, plane, minor)].wait_recv()
                self.seen.add((half, plane, minor))

        def spread_on(self, half, minor):
            self.wait(half, 3, minor)
            self.spread(half, minor)

        def forward(self, half, minor):
            plane, way = (2, 1) if minor < 2 else (1, -1)
            self.wait(half, plane, minor)
            self.move(half, (plane, minor), (0, minor), along(half, major=way))

        def need(self, *chunks):
            for c in chunks:
                for half in (0, 1):
                    for plane, minor in CHUNKS[c]:
                        if (plane, minor) != (3, 0):
                            self.wait(half, plane, minor)

    gather_x, gather_g = Gather(xl), Gather(grads)
    for copy in first_copies:
        copy.wait()
    tile_copies = []

    def send_tiles():
        for copy in small_copies:
            copy.wait()
        tiles[0:8, :] = jnp.full((8, 128), -1.0, F32)
        tiles[0:1, 0:BLOCK] = spots[...].astype(F32)
        tiles[1:2, 0:BLOCK] = parts[...].astype(F32)
        tiles[2:3, 0:BLOCK] = ratios[...]
        for dz, dy in others:
            slot = ((-dz) % 4) * 4 + (-dy) % 4
            tile_copies.append(
                transfer(tiles.at[0:8, :], tiles.at[slot * 8 : slot * 8 + 8, :], device(dz=dz, dy=dy))
            )

    def slot_of(half, plane, minor):
        major, less = PLANE_OFF[plane] % 4, MINOR_OFF[minor] % 4
        return major * 4 + less if half == 0 else less * 4 + major

    def tables():
        for copy in tile_copies:
            copy.wait_recv()
        table = tiles[...]
        turned = table.T
        for half in (0, 1):
            for plane in range(4):
                for minor in range(4):
                    lane = slot_of(half, plane, minor) * 8
                    column = turned[half * HALF : half * HALF + HALF, lane : lane + 1]
                    places[place(half, plane, minor), :] = jnp.broadcast_to(column, (HALF, 128)).astype(jnp.int32)
        segment_part = jnp.concatenate([table[8 * i + 1 : 8 * i + 2, :] for i in range(16)], 0)
        ratio_part = jnp.concatenate([table[8 * i + 2 : 8 * i + 3, :] for i in range(16)], 0)

        def total(s):
            return jnp.sum(jnp.where(segment_part == float(s), ratio_part, 0.0), axis=(0, 1), keepdims=True)

        own_segment = turned[0:BLOCK, 1:2]
        token_weight = jnp.zeros((BLOCK, 1), F32)
        for p in range(4):
            margin = BETA * (total(2 * p) - total(2 * p + 1))
            pair_weight = -BETA * jax.nn.sigmoid(-margin)
            token_weight = jnp.where(own_segment == float(2 * p), pair_weight, token_weight)
            token_weight = jnp.where(own_segment == float(2 * p + 1), -pair_weight, token_weight)
        for half in (0, 1):
            part = rows(half * HALF, HALF)
            weight = token_weight[half * HALF : half * HALF + HALF, :]
            grads[place(half, 3, 0), :] = (weight * token_grad[part, :].astype(F32)).astype(BF16)

    ready = []

    def need_weights():
        if not ready:
            for copy in weight_copies:
                copy.wait()
            ready.append(True)

    def tokens_of(c):
        lane = lax.broadcasted_iota(jnp.int32, (1, CHUNK), 1)
        token = lane
        for j in range(8):
            half, (plane, minor) = j // 4, CHUNKS[c][j % 4]
            major, less = PLANE_OFF[plane], MINOR_OFF[minor]
            dz, dy = (major, less) if half == 0 else (less, major)
            block = lax.rem(z + dz + 4, 4) * 4 + lax.rem(y + dy + 4, 4)
            inside = (lane >= j * HALF) & (lane < (j + 1) * HALF)
            token = token + jnp.where(inside, block * BLOCK + half * HALF - j * HALF, 0)
        return token

    def match(c, first, count, ref):
        token = tokens_of(c)

        def build(i, carry):
            part = rows(pl.multiple_of(i * 128, 128), 128)
            here = places[rows(pl.multiple_of(first + i * 128, 128), 128), 0:1]
            ref[part, :] = jnp.where(here == token, 1.0, 0.0).astype(BF16)
            return carry

        lax.fori_loop(0, count // 128, build, 0)

    def permute_most(c):
        gather_x.need(1, 2, 3)
        match(c, FAR, TOK - FAR, onehot)
        xs[rows(c * CHUNK, CHUNK), :] = lax.dot_general(
            onehot[...], xl[FAR:TOK, :], NT, preferred_element_type=F32
        ).astype(BF16)

    def permute_rest(c):
        gather_x.need(0)
        match(c, 0, FAR, onehot_far)
        chunk = rows(c * CHUNK, CHUNK)
        rest = lax.dot_general(onehot_far[...], xl[0:FAR, :], NT, preferred_element_type=F32)
        xs[chunk, :] = (xs[chunk, :].astype(F32) + rest).astype(BF16)

    def pre_matmul(c, i):
        need_weights()
        chunk, cols = rows(c * CHUNK, CHUNK), rows(i * FB, FB)
        pre[chunk, cols] = jnp.dot(xs[chunk, :], weights[:, cols], preferred_element_type=F32).astype(BF16)
        forward[c].pair_send(i)

    def gh_matmul(c):
        need_weights()
        gather_g.need(c)
        chunk = rows(c * CHUNK, CHUNK)
        ghp[chunk, :] = lax.dot_general(grads[chunk, :], down[...], TN, preferred_element_type=F32).astype(BF16)
        backward[c].pair_send(0)

    def mixed_matmul(c):
        chunk = rows(c * CHUNK, CHUNK)
        forward[c].out_wait()
        part_m[chunk, :] = jnp.dot(hid[chunk, :], down[...], preferred_element_type=F32).astype(BF16)

    def ginp_matmul(c):
        chunk = rows(c * CHUNK, CHUNK)
        backward[c].out_wait()
        if not gather_x.left:
            gather_x.left = True
            for copy in gather_x.got.values():
                copy.wait_send()
                gone.add(id(copy))
        part_i[chunk, :] = lax.dot_general(
            act[chunk, :], weights[...], TN, preferred_element_type=F32
        ).astype(BF16)

    xp, xm, xo = lax.rem(x + 1, 4), lax.rem(x + 3, 4), lax.rem(x + 2, 4)

    class RowChunk:
        def __init__(self, c, part, pair, r1, r2, width, out, out_width):
            self.c, self.part, self.pair, self.r1, self.r2 = c, part, pair, r1, r2
            self.width, self.out, self.out_width = width, out, out_width
            self.pairs, self.far, self.near, self.last = {}, {}, {}, {}

        def cut(self, width):
            if width == 2 * FB:
                return FB
            return 512 if self.c % 2 == 0 else 384

        def mine(self, xx):
            return rows(pl.multiple_of(self.c * CHUNK + k * PLANE + xx * SHARE, 16), SHARE)

        def pair_send(self, i):
            theirs = rows(pl.multiple_of(self.c * CHUNK + (1 - k) * PLANE, 16), PLANE)
            cols = rows(i * FB, FB)
            self.pairs[i] = transfer(self.part.at[theirs, cols], self.pair.at[self.c, :, cols], device(dk=1))

        def pair_add(self, i):
            self.pairs[i].wait_recv()
            mine, cols = rows(pl.multiple_of(self.c * CHUNK + k * PLANE, 16), PLANE), rows(i * FB, FB)
            both = self.part[mine, cols].astype(F32) + self.pair[self.c, :, cols].astype(F32)
            self.part[mine, cols] = both.astype(BF16)
            cut, far = self.cut(self.width), self.mine(xo)
            for way, lo, hi, dx in ((0, 0, cut, 1), (1, cut, self.width, -1)):
                if self.width == FB or way == i:
                    self.far[way] = transfer(
                        self.part.at[far, lo:hi], self.r1.at[self.c, :, lo:hi], device(dx=dx)
                    )

        def ring_add(self, i):
            cut = self.cut(self.width)
            xx, lo, hi, dx = ((xp, 0, cut, 1), (xm, cut, self.width, -1))[i]
            self.far[i].wait_recv()
            mine = self.mine(xx)
            both = self.part[mine, lo:hi].astype(F32) + self.r1[self.c, :, lo:hi].astype(F32)
            self.part[mine, lo:hi] = both.astype(BF16)
            self.near[i] = transfer(self.part.at[mine, :], self.r2.at[self.c, i], device(dx=dx))

        def total(self):
            self.near[0].wait_recv()
            self.near[1].wait_recv()
            return (
                self.part[self.mine(x), :].astype(F32)
                + self.r2[self.c, 0].astype(F32)
                + self.r2[self.c, 1].astype(F32)
            )

        def out_send(self):
            own = self.out.at[self.mine(x), :]
            self.side = [
                transfer(own, own, device(dx=1), self.out.at[self.mine(xm), :]),
                transfer(own, own, device(dx=-1), self.out.at[self.mine(xp), :]),
            ]

        def out_forward(self, i):
            cut = self.cut(self.out_width)
            xx, lo, hi, dx = ((xm, 0, cut, 1), (xp, cut, self.out_width, -1))[i]
            self.side[i].wait_recv()
            piece = self.out.at[self.mine(xx), lo:hi]
            self.last[i] = transfer(piece, piece, device(dx=dx), self.out.at[self.mine(xo), lo:hi])

        def out_pair(self):
            self.last[0].wait_recv()
            self.last[1].wait_recv()
            mine = self.out.at[rows(pl.multiple_of(self.c * CHUNK + k * PLANE, 16), PLANE), :]
            theirs = self.out.at[rows(pl.multiple_of(self.c * CHUNK + (1 - k) * PLANE, 16), PLANE), :]
            self.done = transfer(mine, mine, device(dk=1), theirs)

        def out_wait(self):
            if self.done is not None:
                self.done.wait_recv()
                self.done = None

    forward = [RowChunk(c, pre, pre_pair, pre_r1, pre_r2, 2 * FB, hid, FB) for c in range(4)]
    backward = [RowChunk(c, ghp, gh_pair, gh_r1, gh_r2, FB, act, 2 * FB) for c in range(4)]

    def hidden(c):
        both = forward[c].total()
        pre_share[c] = both
        gate, up = both[:, :FB], both[:, FB:]
        hid[forward[c].mine(x), :] = (gate * jax.nn.sigmoid(gate) * up).astype(BF16)
        forward[c].out_send()

    def acts(c):
        grad = backward[c].total()
        gate, up = pre_share[c, :, 0:FB], pre_share[c, :, FB : 2 * FB]
        s = jax.nn.sigmoid(gate)
        mine = backward[c].mine(x)
        act[mine, 0:FB] = (grad * up * s * (1.0 + gate * (1.0 - s))).astype(BF16)
        act[mine, FB : 2 * FB] = (grad * gate * s).astype(BF16)
        backward[c].out_send()

    class ColSum:
        def __init__(self, half, which, part, out):
            self.half, self.part, self.out = half, part, out
            self.c1, self.c2, self.c3 = c1.at[which], c2.at[which], c3.at[which]

        def part_of(self, c, i):
            return rows(c * CHUNK + self.half * PLANE + i * 96, 96)

        def near_send(self, c, i, way):
            to = 0 if way == 1 else 1
            self.near.append(
                transfer(
                    self.part.at[self.part_of(c, i), :],
                    self.c2.at[to, i * 96 : i * 96 + 96, :],
                    along(self.half, major=way),
                )
            )

        def send_far(self):
            self.far = [
                transfer(self.part.at[self.part_of(0, i), :], self.c1.at[i], along(self.half, major=1 - 2 * i))
                for i in (0, 1)
            ]
            self.near = []

        def send_near(self, i):
            self.far[i].wait_recv()
            mine = self.part_of(1, i)
            self.part[mine, :] = (self.part[mine, :].astype(F32) + self.c1[i].astype(F32)).astype(BF16)
            self.near_send(1, i, 1 - 2 * i)

        def send_rest(self):
            self.near_send(2, 0, -1)
            self.near_send(2, 1, 1)

        def send_minor(self):
            for copy in self.near:
                copy.wait_recv()
            start = 3 * CHUNK + self.half * PLANE
            own = rows(start, PLANE)
            self.part[own, :] = (
                self.part[own, :].astype(F32) + self.c2[0].astype(F32) + self.c2[1].astype(F32)
            ).astype(BF16)
            self.minor = [
                transfer(
                    self.part.at[rows(start + m * HALF, HALF), :],
                    self.c3.at[m - 1],
                    along(self.half, minor=MINOR_OFF[m]),
                )
                for m in (1, 2, 3)
            ]

        def store(self):
            total = self.part[rows(3 * CHUNK + self.half * PLANE, HALF), :].astype(F32)
            for i in range(3):
                self.minor[i].wait_recv()
                total = total + self.c3[i].astype(F32)
            self.out[rows(self.half * HALF, HALF), :] = total.astype(BF16)

    mixed_sum = [ColSum(h, h, part_m, mixed) for h in (0, 1)]
    ginp_sum = [ColSum(h, 2 + h, part_i, ginp) for h in (0, 1)]

    stores = []

    def down_grad(i):
        cols = rows(i * 256, 256)
        gather_g.need(0, 1, 2, 3)
        for c in range(4):
            forward[c].out_wait()
        totals_d[i] = lax.dot_general(hid[...], grads[:, cols], NT, preferred_element_type=F32)
        stores.append(fetch(totals_d.at[i], gdown.at[:, cols]))

    def up_grad(i, first, count):
        cols, part = rows(i % 4 * 256, 256), rows(first * CHUNK, count * CHUNK)
        wide = rows(i // 4 * FB, FB)
        for c in range(first, first + count):
            backward[c].out_wait()
        new = lax.dot_general(xs[part, cols], act[part, wide], NT, preferred_element_type=F32)
        totals_u[cols, wide] = totals_u[cols, wide] + new if first else new

    def up_grad_most(i):
        up_grad(i, 0, 3)

    def up_grad_rest(i):
        up_grad(i, 3, 1)
        cols = rows(i % 4 * 256, 256)
        stores.append(fetch(totals_u.at[cols, rows(i // 4 * FB, FB)], (ggate, gup)[i // 4].at[cols, :]))

    gather_x.begin()
    send_tiles()
    gather_x.forward(0, 0)
    gather_x.spread_on(0, 2)
    gather_x.spread_on(0, 1)
    gather_x.spread_on(1, 1)
    gather_x.spread_on(1, 2)
    gather_x.spread_on(0, 3)
    gather_x.forward(1, 0)
    gather_x.spread_on(1, 3)
    tables()
    gather_x.forward(1, 1)
    gather_x.forward(0, 2)
    gather_x.forward(1, 2)
    gather_x.forward(0, 3)
    gather_x.forward(1, 3)
    gather_x.forward(0, 1)
    gather_g.begin()
    permute_most(2)
    permute_most(0)
    permute_rest(0)
    pre_matmul(0, 0)
    gather_g.spread_on(0, 2)
    gather_g.spread_on(0, 1)
    gather_g.forward(0, 0)
    pre_matmul(0, 1)
    forward[0].pair_add(0)
    gather_g.spread_on(1, 2)
    gather_g.spread_on(1, 1)
    gather_g.spread_on(0, 3)
    permute_rest(2)
    forward[0].pair_add(1)
    permute_most(1)
    gather_g.spread_on(1, 3)
    gather_g.forward(1, 0)
    forward[0].ring_add(0)
    permute_rest(1)
    gather_g.forward(0, 2)
    gather_g.forward(1, 2)
    pre_matmul(1, 0)
    forward[0].ring_add(1)
    pre_matmul(1, 1)
    gather_g.forward(1, 1)
    gather_g.forward(0, 1)
    forward[1].pair_add(0)
    gh_matmul(3)
    gather_g.forward(0, 3)
    forward[1].pair_add(1)
    gather_g.forward(1, 3)
    gh_matmul(2)
    gh_matmul(1)
    forward[1].ring_add(0)
    hidden(0)
    backward[2].pair_add(0)
    pre_matmul(2, 1)
    gh_matmul(0)
    backward[1].pair_add(0)
    forward[1].ring_add(1)
    forward[2].pair_add(1)
    backward[3].pair_add(0)
    forward[0].out_forward(1)
    backward[0].pair_add(0)
    backward[2].ring_add(1)
    pre_matmul(2, 0)
    backward[1].ring_add(1)
    permute_most(3)
    forward[2].pair_add(0)
    backward[2].ring_add(0)
    permute_rest(3)
    backward[1].ring_add(0)
    forward[0].out_forward(0)
    hidden(1)
    backward[3].ring_add(0)
    pre_matmul(3, 0)
    backward[0].ring_add(0)
    forward[2].ring_add(1)
    pre_matmul(3, 1)
    backward[3].ring_add(1)
    forward[3].pair_add(0)
    forward[2].ring_add(0)
    backward[0].ring_add(1)
    forward[3].pair_add(1)
    forward[0].out_pair()
    acts(1)
    mixed_matmul(0)
    mixed_sum[1].send_far()
    forward[1].out_forward(1)
    forward[1].out_forward(0)
    mixed_sum[0].send_far()
    forward[3].ring_add(0)
    acts(0)
    hidden(2)
    acts(2)
    forward[3].ring_add(1)
    backward[1].out_forward(0)
    backward[1].out_forward(1)
    forward[1].out_pair()
    mixed_matmul(1)
    mixed_sum[0].send_near(1)
    mixed_sum[1].send_near(1)
    mixed_sum[0].send_near(0)
    mixed_sum[1].send_near(0)
    backward[0].out_forward(1)
    forward[2].out_forward(1)
    backward[0].out_forward(0)
    forward[2].out_forward(0)
    backward[2].out_forward(1)
    backward[2].out_forward(0)
    hidden(3)
    acts(3)
    backward[1].out_pair()
    backward[0].out_pair()
    ginp_matmul(1)
    ginp_matmul(0)
    ginp_sum[0].send_far()
    forward[2].out_pair()
    ginp_sum[1].send_far()
    backward[2].out_pair()
    forward[3].out_forward(0)
    forward[3].out_forward(1)
    mixed_matmul(2)
    mixed_sum[1].send_rest()
    mixed_sum[0].send_rest()
    ginp_matmul(2)
    backward[3].out_forward(0)
    backward[3].out_forward(1)
    ginp_sum[1].send_rest()
    ginp_sum[0].send_rest()
    forward[3].out_pair()
    up_grad_most(2)
    ginp_sum[1].send_near(1)
    ginp_sum[0].send_near(1)
    ginp_sum[1].send_near(0)
    mixed_matmul(3)
    ginp_sum[0].send_near(0)
    down_grad(3)
    down_grad(2)
    mixed_sum[1].send_minor()
    mixed_sum[0].send_minor()
    backward[3].out_pair()
    up_grad_most(0)
    up_grad_most(1)
    down_grad(1)
    ginp_matmul(3)
    up_grad_rest(0)
    up_grad_rest(1)
    up_grad_most(3)
    up_grad_most(6)
    ginp_sum[1].send_minor()
    ginp_sum[0].send_minor()
    up_grad_most(7)
    down_grad(0)
    up_grad_rest(2)
    up_grad_rest(3)
    mixed_sum[1].store()
    mixed_sum[0].store()
    up_grad_rest(6)
    up_grad_most(5)
    up_grad_rest(5)
    up_grad_rest(7)
    up_grad_most(4)
    up_grad_rest(4)
    ginp_sum[1].store()
    ginp_sum[0].store()
    for copy in stores:
        copy.wait()
    for copy in sent:
        if id(copy) not in gone:
            copy.wait_send()


COPIES = 26


def hand_over(*refs):
    come, go = refs[15:17]
    moves = []
    for n, (src, dst) in enumerate(zip(refs[:5], refs[5:10])):
        pieces = 8 if n > 1 else 1
        size = src.shape[0] // pieces
        held = refs[10 + n]
        for i in range(pieces):
            part, index = rows(i * size, size), len(moves)
            moves.append(
                (
                    pltpu.make_async_copy(src.at[part, :], held.at[part, :], come.at[index]),
                    pltpu.make_async_copy(held.at[part, :], dst.at[part, :], go.at[index]),
                )
            )
    for arrive, _ in moves:
        arrive.start()
    for arrive, leave in moves:
        arrive.wait()
        leave.start()
    for _, leave in moves:
        leave.wait()


def per_device(loaded, positions, gate_weight, up_weight, down_weight, segment, log_ratio, token_grad):
    vmem, anywhere = pl.BlockSpec(memory_space=pltpu.VMEM), pl.BlockSpec(memory_space=pl.ANY)
    shape = jax.ShapeDtypeStruct
    buf = lambda *s: pltpu.VMEM(s, BF16)
    transfers = 200
    scratch = [
        pltpu.VMEM((128, 128), F32),
        buf(DB, 2 * FB),
        buf(FB, DB),
        buf(TOK, DB),
        buf(TOK, DB),
        buf(TOK, DB),
        buf(TOK, 2 * FB),
        buf(4, PLANE, 2 * FB),
        buf(4, SHARE, 2 * FB),
        buf(4, 2, SHARE, 2 * FB),
        pltpu.VMEM((4, SHARE, 2 * FB), F32),
        buf(TOK, FB),
        buf(TOK, FB),
        buf(4, PLANE, FB),
        buf(4, SHARE, FB),
        buf(4, 2, SHARE, FB),
        buf(TOK, 2 * FB),
        buf(TOK, DB),
        buf(4, 2, 96, DB),
        buf(4, 2, PLANE, DB),
        buf(4, 3, HALF, DB),
        buf(TOK - FAR, CHUNK),
        buf(FAR, CHUNK),
        pltpu.VMEM((TOK, 128), jnp.int32),
        pltpu.VMEM((DB, 2 * FB), F32),
        pltpu.VMEM((4, FB, 256), F32),
        pltpu.VMEM((1, BLOCK), jnp.int32),
        pltpu.VMEM((1, BLOCK), jnp.int32),
        pltpu.VMEM((1, BLOCK), F32),
        buf(BLOCK, DB),
        pltpu.SemaphoreType.DMA((transfers,)),
        pltpu.SemaphoreType.DMA((transfers,)),
        pltpu.SemaphoreType.DMA((32,)),
    ]
    outs = pl.pallas_call(
        kernel,
        out_shape=(
            shape((BLOCK, DB), BF16),
            shape((BLOCK, DB), BF16),
            shape((DB, FB), F32),
            shape((DB, FB), F32),
            shape((FB, DB), F32),
        ),
        in_specs=[anywhere] * 8,
        out_specs=[vmem] * 2 + [anywhere] * 3,
        scratch_shapes=scratch,
        compiler_params=pltpu.CompilerParams(
            collective_id=0, has_side_effects=True, vmem_limit_bytes=64 * 1024 * 1024
        ),
        name="feed_forward",
    )(
        positions.reshape(1, BLOCK), segment.reshape(1, BLOCK), log_ratio.reshape(1, BLOCK),
        loaded, token_grad, gate_weight, up_weight, down_weight,
    )
    return pl.pallas_call(
        hand_over,
        out_shape=tuple(shape(o.shape, o.dtype) for o in outs),
        in_specs=[anywhere] * 5,
        out_specs=[anywhere] * 5,
        scratch_shapes=[pltpu.VMEM(o.shape, o.dtype) for o in outs]
        + [pltpu.SemaphoreType.DMA((COPIES,)), pltpu.SemaphoreType.DMA((COPIES,))],
        compiler_params=pltpu.CompilerParams(vmem_limit_bytes=32 * 1024 * 1024),
        name="hand_over",
    )(*outs)


def solution(mesh):
    return jax.shard_map(
        per_device,
        mesh=mesh,
        in_specs=(
            P("col", "row"),
            P("col"),
            P("row", "col"),
            P("row", "col"),
            P("col", "row"),
            P("col"),
            P("col"),
            P("col", "row"),
        ),
        out_specs=(
            P("col", "row"),
            P("col", "row"),
            P("row", "col"),
            P("row", "col"),
            P("col", "row"),
        ),
        check_vma=False,
    )
```

```python
import jax
import jax.numpy as jnp
from jax import lax
from jax.experimental import pallas as pl
from jax.experimental.pallas import tpu as pltpu
from jax.sharding import PartitionSpec as P

BETA = 0.1
F32, BF16 = jnp.float32, jnp.bfloat16
TOK, DB, FB = 1536, 1024, 896
BLOCK, HALF = 96, 48
CHUNK, SHARE = 384, 48
PLANE = 192
FAR = 384
PLANE_OFF = (2, 1, -1, 0)
MINOR_OFF = (0, 1, -1, 2)
CHUNKS = (
    ((0, 0), (0, 1), (0, 2), (0, 3)),
    ((1, 0), (1, 1), (2, 2), (2, 3)),
    ((2, 0), (2, 1), (1, 2), (1, 3)),
    ((3, 0), (3, 1), (3, 2), (3, 3)),
)
NT = (((0,), (0,)), ((), ()))
TN = (((1,), (1,)), ((), ()))


def rows(start, size):
    return pl.ds(start, size)


def kernel(spots, parts, ratios, loaded, token_grad, gw, uw, dw, mixed, ginp, ggate, gup, gdown, *scratch):
    (tiles, weights, down, xl, xs, grads, pre, pre_pair, pre_r1, pre_r2, pre_share, hid, ghp, gh_pair,
     gh_r1, gh_r2, act, part_m, c1, c2, c3, onehot, onehot_far, places, totals_u, totals_d, small_u, small_s, small_f, held_grad, send, recv, local) = scratch
    part_i = xl
    row, col = lax.axis_index("row"), lax.axis_index("col")
    x, k, z, y = row // 2, row % 2, col // 4, col % 4

    def device(dx=0, dk=0, dz=0, dy=0):
        return {
            "row": lax.rem(x + dx + 4, 4) * 2 + lax.rem(k + dk, 2),
            "col": lax.rem(z + dz + 4, 4) * 4 + lax.rem(y + dy + 4, 4),
        }

    sent, gone = [], set()

    def transfer(src, dst, target, landing=None):
        index = len(sent)
        copy = pltpu.make_async_remote_copy(
            src_ref=src, dst_ref=dst, send_sem=send.at[index], recv_sem=recv.at[index],
            device_id=target, device_id_type=pl.DeviceIdType.MESH,
        )
        copy.start()
        sent.append(copy)
        if landing is None:
            return copy
        return pltpu.make_async_remote_copy(
            src_ref=src, dst_ref=landing, send_sem=send.at[index], recv_sem=recv.at[index],
            device_id=target, device_id_type=pl.DeviceIdType.MESH,
        )

    local_copies = []

    def fetch(src, dst):
        copy = pltpu.make_async_copy(src, dst, local.at[len(local_copies)])
        copy.start()
        local_copies.append(copy)
        return copy

    def along(half, major=0, minor=0):
        return device(dz=major, dy=minor) if half == 0 else device(dz=minor, dy=major)

    def place(half, plane, minor):
        for c, held in enumerate(CHUNKS):
            if (plane, minor) in held:
                return rows(c * CHUNK + half * PLANE + held.index((plane, minor)) * HALF, HALF)

    sources = (spots, parts, ratios, token_grad)
    spots, parts, ratios, token_grad = small_u, small_s, small_f, held_grad
    first_copies = [
        fetch(loaded.at[rows(half * HALF, HALF), :], xl.at[place(half, 3, 0), :]) for half in (0, 1)
    ]
    small_copies = [fetch(a, b) for a, b in zip(sources, (spots, parts, ratios, token_grad))]
    weight_copies = [fetch(gw, weights.at[:, 0:FB]), fetch(uw, weights.at[:, FB : 2 * FB]), fetch(dw, down)]

    others = [(dz, dy) for dz in range(4) for dy in range(4) if (dz, dy) != (0, 0)]
    barrier = pltpu.get_barrier_semaphore()
    peers = [device(dz=dz, dy=dy) for dz, dy in others]
    peers += [device(dx=1), device(dx=-1), device(dk=1)]
    for peer in peers:
        pl.semaphore_signal(barrier, inc=1, device_id=peer, device_id_type=pl.DeviceIdType.MESH)
    pl.semaphore_wait(barrier, len(peers))

    class Gather:
        def __init__(self, buf):
            self.buf, self.got, self.seen, self.left = buf, {}, set(), False

        def move(self, half, src, dst, target):
            self.got[(half,) + dst] = transfer(
                self.buf.at[place(half, *src)], self.buf.at[place(half, *dst)], target
            )

        def spread(self, half, minor):
            self.move(half, (3, minor), (2, minor), along(half, major=1))
            self.move(half, (3, minor), (1, minor), along(half, major=-1))

        def begin(self):
            for half in (0, 1):
                self.move(half, (3, 0), (3, 2), along(half, minor=1))
                self.move(half, (3, 0), (3, 1), along(half, minor=-1))
                self.move(half, (3, 0), (3, 3), along(half, minor=2))
                self.spread(half, 0)

        def wait(self, half, plane, minor):
            if (half, plane, minor) not in self.seen:
                self.got[(half, plane, minor)].wait_recv()
                self.seen.add((half, plane, minor))

        def spread_on(self, half, minor):
            self.wait(half, 3, minor)
            self.spread(half, minor)

        def forward(self, half, minor):
            plane, way = (2, 1) if minor < 2 else (1, -1)
            self.wait(half, plane, minor)
            self.move(half, (plane, minor), (0, minor), along(half, major=way))

        def need(self, *chunks):
            for c in chunks:
                for half in (0, 1):
                    for plane, minor in CHUNKS[c]:
                        if (plane, minor) != (3, 0):
                            self.wait(half, plane, minor)

    gather_x, gather_g = Gather(xl), Gather(grads)
    for copy in first_copies:
        copy.wait()
    tile_copies = []

    def send_tiles():
        for copy in small_copies:
            copy.wait()
        tiles[0:8, :] = jnp.full((8, 128), -1.0, F32)
        tiles[0:1, 0:BLOCK] = spots[...].astype(F32)
        tiles[1:2, 0:BLOCK] = parts[...].astype(F32)
        tiles[2:3, 0:BLOCK] = ratios[...]
        for dz, dy in others:
            slot = ((-dz) % 4) * 4 + (-dy) % 4
            tile_copies.append(
                transfer(tiles.at[0:8, :], tiles.at[slot * 8 : slot * 8 + 8, :], device(dz=dz, dy=dy))
            )

    def slot_of(half, plane, minor):
        major, less = PLANE_OFF[plane] % 4, MINOR_OFF[minor] % 4
        return major * 4 + less if half == 0 else less * 4 + major

    def tables():
        for copy in tile_copies:
            copy.wait_recv()
        table = tiles[...]
        turned = table.T
        for half in (0, 1):
            for plane in range(4):
                for minor in range(4):
                    lane = slot_of(half, plane, minor) * 8
                    column = turned[half * HALF : half * HALF + HALF, lane : lane + 1]
                    places[place(half, plane, minor), :] = jnp.broadcast_to(column, (HALF, 128)).astype(jnp.int32)
        segment_part = jnp.concatenate([table[8 * i + 1 : 8 * i + 2, :] for i in range(16)], 0)
        ratio_part = jnp.concatenate([table[8 * i + 2 : 8 * i + 3, :] for i in range(16)], 0)

        def total(s):
            return jnp.sum(jnp.where(segment_part == float(s), ratio_part, 0.0), axis=(0, 1), keepdims=True)

        own_segment = turned[0:BLOCK, 1:2]
        token_weight = jnp.zeros((BLOCK, 1), F32)
        for p in range(4):
            margin = BETA * (total(2 * p) - total(2 * p + 1))
            pair_weight = -BETA * jax.nn.sigmoid(-margin)
            token_weight = jnp.where(own_segment == float(2 * p), pair_weight, token_weight)
            token_weight = jnp.where(own_segment == float(2 * p + 1), -pair_weight, token_weight)
        for half in (0, 1):
            part = rows(half * HALF, HALF)
            weight = token_weight[half * HALF : half * HALF + HALF, :]
            grads[place(half, 3, 0), :] = (weight * token_grad[part, :].astype(F32)).astype(BF16)

    ready = []

    def need_weights():
        if not ready:
            for copy in weight_copies:
                copy.wait()
            ready.append(True)

    def tokens_of(c):
        lane = lax.broadcasted_iota(jnp.int32, (1, CHUNK), 1)
        token = lane
        for j in range(8):
            half, (plane, minor) = j // 4, CHUNKS[c][j % 4]
            major, less = PLANE_OFF[plane], MINOR_OFF[minor]
            dz, dy = (major, less) if half == 0 else (less, major)
            block = lax.rem(z + dz + 4, 4) * 4 + lax.rem(y + dy + 4, 4)
            inside = (lane >= j * HALF) & (lane < (j + 1) * HALF)
            token = token + jnp.where(inside, block * BLOCK + half * HALF - j * HALF, 0)
        return token

    def match(c, first, count, ref):
        token = tokens_of(c)

        def build(i, carry):
            part = rows(pl.multiple_of(i * 128, 128), 128)
            here = places[rows(pl.multiple_of(first + i * 128, 128), 128), :]
            for j in range(0, CHUNK, 128):
                ref[part, j : j + 128] = jnp.where(here == token[:, j : j + 128], 1.0, 0.0).astype(BF16)
            return carry

        lax.fori_loop(0, count // 128, build, 0)

    def permute_most(c):
        gather_x.need(1, 2, 3)
        match(c, FAR, TOK - FAR, onehot)
        xs[rows(c * CHUNK, CHUNK), :] = lax.dot_general(
            onehot[...], xl[FAR:TOK, :], NT, preferred_element_type=F32
        ).astype(BF16)

    def permute_rest(c):
        gather_x.need(0)
        match(c, 0, FAR, onehot_far)
        chunk = rows(c * CHUNK, CHUNK)
        rest = lax.dot_general(onehot_far[...], xl[0:FAR, :], NT, preferred_element_type=F32)
        xs[chunk, :] = (xs[chunk, :].astype(F32) + rest).astype(BF16)

    def pre_matmul(c, i):
        need_weights()
        chunk, cols = rows(c * CHUNK, CHUNK), rows(i * FB, FB)
        pre[chunk, cols] = jnp.dot(xs[chunk, :], weights[:, cols], preferred_element_type=F32).astype(BF16)
        forward[c].pair_send(i)

    def gh_matmul(c):
        need_weights()
        gather_g.need(c)
        chunk = rows(c * CHUNK, CHUNK)
        ghp[chunk, :] = lax.dot_general(grads[chunk, :], down[...], TN, preferred_element_type=F32).astype(BF16)
        backward[c].pair_send(0)

    def mixed_matmul(c):
        chunk = rows(c * CHUNK, CHUNK)
        forward[c].out_wait()
        part_m[chunk, :] = jnp.dot(hid[chunk, :], down[...], preferred_element_type=F32).astype(BF16)

    def ginp_matmul(c):
        chunk = rows(c * CHUNK, CHUNK)
        backward[c].out_wait()
        if not gather_x.left:
            gather_x.left = True
            for copy in gather_x.got.values():
                copy.wait_send()
                gone.add(id(copy))
        part_i[chunk, :] = lax.dot_general(
            act[chunk, :], weights[...], TN, preferred_element_type=F32
        ).astype(BF16)

    xp, xm, xo = lax.rem(x + 1, 4), lax.rem(x + 3, 4), lax.rem(x + 2, 4)

    class RowChunk:
        def __init__(self, c, part, pair, r1, r2, width, out, out_width):
            self.c, self.part, self.pair, self.r1, self.r2 = c, part, pair, r1, r2
            self.width, self.out, self.out_width = width, out, out_width
            self.pairs, self.far, self.near, self.last = {}, {}, {}, {}

        def cut(self, width):
            if width == 2 * FB:
                return FB
            return 512 if self.c % 2 == 0 else 384

        def mine(self, xx):
            return rows(pl.multiple_of(self.c * CHUNK + k * PLANE + xx * SHARE, 16), SHARE)

        def pair_send(self, i):
            theirs = rows(pl.multiple_of(self.c * CHUNK + (1 - k) * PLANE, 16), PLANE)
            cols = rows(i * FB, FB)
            self.pairs[i] = transfer(self.part.at[theirs, cols], self.pair.at[self.c, :, cols], device(dk=1))

        def pair_add(self, i):
            self.pairs[i].wait_recv()
            mine, cols = rows(pl.multiple_of(self.c * CHUNK + k * PLANE, 16), PLANE), rows(i * FB, FB)
            both = self.part[mine, cols].astype(F32) + self.pair[self.c, :, cols].astype(F32)
            self.part[mine, cols] = both.astype(BF16)
            cut, far = self.cut(self.width), self.mine(xo)
            for way, lo, hi, dx in ((0, 0, cut, 1), (1, cut, self.width, -1)):
                if self.width == FB or way == i:
                    self.far[way] = transfer(
                        self.part.at[far, lo:hi], self.r1.at[self.c, :, lo:hi], device(dx=dx)
                    )

        def ring_add(self, i):
            cut = self.cut(self.width)
            xx, lo, hi, dx = ((xp, 0, cut, 1), (xm, cut, self.width, -1))[i]
            self.far[i].wait_recv()
            mine = self.mine(xx)
            both = self.part[mine, lo:hi].astype(F32) + self.r1[self.c, :, lo:hi].astype(F32)
            self.part[mine, lo:hi] = both.astype(BF16)
            self.near[i] = transfer(self.part.at[mine, :], self.r2.at[self.c, i], device(dx=dx))

        def total(self):
            self.near[0].wait_recv()
            self.near[1].wait_recv()
            return (
                self.part[self.mine(x), :].astype(F32)
                + self.r2[self.c, 0].astype(F32)
                + self.r2[self.c, 1].astype(F32)
            )

        def out_send(self):
            own = self.out.at[self.mine(x), :]
            self.side = [
                transfer(own, own, device(dx=1), self.out.at[self.mine(xm), :]),
                transfer(own, own, device(dx=-1), self.out.at[self.mine(xp), :]),
            ]
            self.done = []
            self.over(x)

        def over(self, xx):
            mine = self.out.at[self.mine(xx), :]
            other = rows(pl.multiple_of(self.c * CHUNK + (1 - k) * PLANE + xx * SHARE, 16), SHARE)
            self.done.append(transfer(mine, mine, device(dk=1), self.out.at[other, :]))

        def out_forward(self, i):
            cut = self.cut(self.out_width)
            xx, lo, hi, dx = ((xm, 0, cut, 1), (xp, cut, self.out_width, -1))[i]
            self.side[i].wait_recv()
            piece = self.out.at[self.mine(xx), lo:hi]
            self.last[i] = transfer(piece, piece, device(dx=dx), self.out.at[self.mine(xo), lo:hi])
            self.over(xx)

        def out_pair(self):
            self.last[0].wait_recv()
            self.last[1].wait_recv()
            self.over(xo)

        def out_wait(self):
            for copy in self.done:
                copy.wait_recv()
            self.done = []

    forward = [RowChunk(c, pre, pre_pair, pre_r1, pre_r2, 2 * FB, hid, FB) for c in range(4)]
    backward = [RowChunk(c, ghp, gh_pair, gh_r1, gh_r2, FB, act, 2 * FB) for c in range(4)]

    def hidden(c):
        both = forward[c].total()
        pre_share[c] = both
        gate, up = both[:, :FB], both[:, FB:]
        hid[forward[c].mine(x), :] = (gate * jax.nn.sigmoid(gate) * up).astype(BF16)
        forward[c].out_send()

    def acts(c):
        grad = backward[c].total()
        gate, up = pre_share[c, :, 0:FB], pre_share[c, :, FB : 2 * FB]
        s = jax.nn.sigmoid(gate)
        mine = backward[c].mine(x)
        act[mine, 0:FB] = (grad * up * s * (1.0 + gate * (1.0 - s))).astype(BF16)
        act[mine, FB : 2 * FB] = (grad * gate * s).astype(BF16)
        backward[c].out_send()

    class ColSum:
        def __init__(self, half, which, part, out):
            self.half, self.part, self.out = half, part, out
            self.c1, self.c2, self.c3 = c1.at[which], c2.at[which], c3.at[which]

        def part_of(self, c, i):
            return rows(c * CHUNK + self.half * PLANE + i * 96, 96)

        def near_send(self, c, i, way):
            to = 0 if way == 1 else 1
            self.near.append(
                transfer(
                    self.part.at[self.part_of(c, i), :],
                    self.c2.at[to, i * 96 : i * 96 + 96, :],
                    along(self.half, major=way),
                )
            )

        def send_far(self):
            self.far = [
                transfer(self.part.at[self.part_of(0, i), :], self.c1.at[i], along(self.half, major=1 - 2 * i))
                for i in (0, 1)
            ]
            self.near = []

        def send_near(self, i):
            self.far[i].wait_recv()
            mine = self.part_of(1, i)
            self.part[mine, :] = (self.part[mine, :].astype(F32) + self.c1[i].astype(F32)).astype(BF16)
            self.near_send(1, i, 1 - 2 * i)

        def send_rest(self):
            self.near_send(2, 0, -1)
            self.near_send(2, 1, 1)

        def send_minor(self):
            for copy in self.near:
                copy.wait_recv()
            start = 3 * CHUNK + self.half * PLANE
            own = rows(start, PLANE)
            self.part[own, :] = (
                self.part[own, :].astype(F32) + self.c2[0].astype(F32) + self.c2[1].astype(F32)
            ).astype(BF16)
            self.minor = [
                transfer(
                    self.part.at[rows(start + m * HALF, HALF), :],
                    self.c3.at[m - 1],
                    along(self.half, minor=MINOR_OFF[m]),
                )
                for m in (1, 2, 3)
            ]

        def store(self):
            total = self.part[rows(3 * CHUNK + self.half * PLANE, HALF), :].astype(F32)
            for i in range(3):
                self.minor[i].wait_recv()
                total = total + self.c3[i].astype(F32)
            self.out[rows(self.half * HALF, HALF), :] = total.astype(BF16)

    mixed_sum = [ColSum(h, h, part_m, mixed) for h in (0, 1)]
    ginp_sum = [ColSum(h, 2 + h, part_i, ginp) for h in (0, 1)]

    stores = []

    def down_grad(i, first):
        cols, part = rows(i * 256, 256), rows(first * CHUNK, 2 * CHUNK)
        gather_g.need(first, first + 1)
        for c in (first, first + 1):
            forward[c].out_wait()
        new = lax.dot_general(hid[part, :], grads[part, cols], NT, preferred_element_type=F32)
        totals_d[i] = totals_d[i] + new if first else new

    def up_grad(i, first):
        cols, part = rows(i % 4 * 256, 256), rows(first * CHUNK, 2 * CHUNK)
        wide = rows(i // 4 * FB, FB)
        for c in (first, first + 1):
            backward[c].out_wait()
        new = lax.dot_general(xs[part, cols], act[part, wide], NT, preferred_element_type=F32)
        totals_u[cols, wide] = totals_u[cols, wide] + new if first else new

    def down_grad_first(i):
        down_grad(i, 0)

    def down_grad_last(i):
        down_grad(i, 2)
        stores.append(fetch(totals_d.at[i], gdown.at[:, rows(i * 256, 256)]))

    def up_grad_first(i):
        up_grad(i, 0)

    def up_grad_last(i):
        up_grad(i, 2)
        cols = rows(i % 4 * 256, 256)
        stores.append(fetch(totals_u.at[cols, rows(i // 4 * FB, FB)], (ggate, gup)[i // 4].at[cols, :]))

    gather_x.begin()
    send_tiles()
    gather_x.spread_on(0, 2)
    gather_x.forward(0, 0)
    gather_x.spread_on(0, 1)
    gather_x.spread_on(1, 2)
    gather_x.spread_on(0, 3)
    gather_x.spread_on(1, 1)
    gather_x.forward(1, 0)
    gather_x.spread_on(1, 3)
    tables()
    gather_x.forward(0, 2)
    gather_x.forward(1, 2)
    gather_x.forward(1, 1)
    gather_x.forward(0, 1)
    gather_x.forward(1, 3)
    gather_x.forward(0, 3)
    gather_g.begin()
    permute_most(0)
    permute_most(1)
    permute_rest(1)
    pre_matmul(1, 0)
    gather_g.spread_on(0, 1)
    gather_g.forward(0, 0)
    pre_matmul(1, 1)
    gather_g.spread_on(1, 2)
    gather_g.spread_on(1, 1)
    forward[1].pair_add(0)
    gather_g.spread_on(0, 2)
    gather_g.spread_on(0, 3)
    permute_rest(0)
    forward[1].pair_add(1)
    pre_matmul(0, 1)
    gather_g.forward(1, 0)
    gather_g.spread_on(1, 3)
    pre_matmul(0, 0)
    forward[1].ring_add(0)
    forward[0].pair_add(1)
    gather_g.forward(1, 2)
    gather_g.forward(0, 1)
    gh_matmul(3)
    forward[0].pair_add(0)
    gather_g.forward(0, 2)
    forward[1].ring_add(1)
    gather_g.forward(1, 1)
    permute_most(2)
    gather_g.forward(1, 3)
    gather_g.forward(0, 3)
    forward[0].ring_add(1)
    backward[3].pair_add(0)
    gh_matmul(2)
    permute_rest(2)
    pre_matmul(2, 1)
    forward[0].ring_add(0)
    pre_matmul(2, 0)
    gh_matmul(0)
    backward[3].ring_add(0)
    backward[2].pair_add(0)
    forward[2].pair_add(0)
    forward[2].pair_add(1)
    gh_matmul(1)
    backward[0].pair_add(0)
    hidden(1)
    backward[3].ring_add(1)
    permute_most(3)
    backward[2].ring_add(1)
    hidden(0)
    forward[2].ring_add(1)
    backward[1].pair_add(0)
    permute_rest(3)
    pre_matmul(3, 0)
    backward[0].ring_add(1)
    pre_matmul(3, 1)
    backward[2].ring_add(0)
    backward[0].ring_add(0)
    forward[2].ring_add(0)
    forward[3].pair_add(0)
    forward[1].out_forward(1)
    forward[3].pair_add(1)
    forward[1].out_forward(0)
    forward[0].out_forward(0)
    backward[1].ring_add(0)
    forward[0].out_forward(1)
    backward[1].ring_add(1)
    acts(0)
    hidden(2)
    acts(2)
    forward[3].ring_add(0)
    forward[3].ring_add(1)
    forward[1].out_pair()
    forward[0].out_pair()
    mixed_matmul(1)
    mixed_matmul(0)
    down_grad_first(3)
    acts(1)
    mixed_sum[1].send_far()
    down_grad_first(2)
    down_grad_first(0)
    mixed_sum[0].send_far()
    backward[0].out_forward(1)
    down_grad_first(1)
    backward[0].out_forward(0)
    forward[2].out_forward(1)
    forward[2].out_forward(0)
    mixed_sum[1].send_near(1)
    mixed_sum[1].send_near(0)
    backward[2].out_forward(1)
    mixed_sum[0].send_near(0)
    mixed_sum[0].send_near(1)
    backward[2].out_forward(0)
    hidden(3)
    acts(3)
    backward[1].out_forward(1)
    backward[1].out_forward(0)
    backward[0].out_pair()
    forward[2].out_pair()
    ginp_matmul(0)
    backward[2].out_pair()
    ginp_sum[0].send_far()
    ginp_sum[1].send_far()
    mixed_matmul(2)
    ginp_matmul(2)
    ginp_sum[1].send_rest()
    ginp_sum[0].send_rest()
    mixed_sum[1].send_rest()
    mixed_sum[0].send_rest()
    forward[3].out_forward(0)
    forward[3].out_forward(1)
    backward[3].out_forward(1)
    backward[3].out_forward(0)
    backward[1].out_pair()
    forward[3].out_pair()
    up_grad_first(1)
    ginp_matmul(1)
    backward[3].out_pair()
    ginp_sum[0].send_near(0)
    ginp_sum[1].send_near(0)
    ginp_sum[0].send_near(1)
    ginp_sum[1].send_near(1)
    down_grad_last(2)
    ginp_matmul(3)
    up_grad_last(1)
    down_grad_last(0)
    down_grad_last(1)
    mixed_matmul(3)
    mixed_sum[1].send_minor()
    mixed_sum[0].send_minor()
    up_grad_first(0)
    up_grad_last(0)
    ginp_sum[0].send_minor()
    ginp_sum[1].send_minor()
    down_grad_last(3)
    up_grad_first(3)
    up_grad_last(3)
    up_grad_first(4)
    up_grad_last(4)
    up_grad_first(5)
    up_grad_last(5)
    mixed_sum[0].store()
    mixed_sum[1].store()
    up_grad_first(2)
    up_grad_last(2)
    up_grad_first(7)
    up_grad_last(7)
    up_grad_first(6)
    up_grad_last(6)
    ginp_sum[0].store()
    ginp_sum[1].store()
    for copy in stores:
        copy.wait()
    for copy in sent:
        if id(copy) not in gone:
            copy.wait_send()


STEPS = 4


def hand_over(*refs):
    for src, dst in zip(refs[:5], refs[5:]):
        dst[...] = src[...]


def per_device(loaded, positions, gate_weight, up_weight, down_weight, segment, log_ratio, token_grad):
    vmem, anywhere = pl.BlockSpec(memory_space=pltpu.VMEM), pl.BlockSpec(memory_space=pl.ANY)
    shape = jax.ShapeDtypeStruct
    buf = lambda *s: pltpu.VMEM(s, BF16)
    transfers = 220
    scratch = [
        pltpu.VMEM((128, 128), F32),
        buf(DB, 2 * FB),
        buf(FB, DB),
        buf(TOK, DB),
        buf(TOK, DB),
        buf(TOK, DB),
        buf(TOK, 2 * FB),
        buf(4, PLANE, 2 * FB),
        buf(4, SHARE, 2 * FB),
        buf(4, 2, SHARE, 2 * FB),
        pltpu.VMEM((4, SHARE, 2 * FB), F32),
        buf(TOK, FB),
        buf(TOK, FB),
        buf(4, PLANE, FB),
        buf(4, SHARE, FB),
        buf(4, 2, SHARE, FB),
        buf(TOK, 2 * FB),
        buf(TOK, DB),
        buf(4, 2, 96, DB),
        buf(4, 2, PLANE, DB),
        buf(4, 3, HALF, DB),
        buf(TOK - FAR, CHUNK),
        buf(FAR, CHUNK),
        pltpu.VMEM((TOK, 128), jnp.int32),
        pltpu.VMEM((DB, 2 * FB), F32),
        pltpu.VMEM((4, FB, 256), F32),
        pltpu.VMEM((1, BLOCK), jnp.int32),
        pltpu.VMEM((1, BLOCK), jnp.int32),
        pltpu.VMEM((1, BLOCK), F32),
        buf(BLOCK, DB),
        pltpu.SemaphoreType.DMA((transfers,)),
        pltpu.SemaphoreType.DMA((transfers,)),
        pltpu.SemaphoreType.DMA((32,)),
    ]
    outs = pl.pallas_call(
        kernel,
        out_shape=(
            shape((BLOCK, DB), BF16),
            shape((BLOCK, DB), BF16),
            shape((DB, FB), F32),
            shape((DB, FB), F32),
            shape((FB, DB), F32),
        ),
        in_specs=[anywhere] * 8,
        out_specs=[vmem] * 2 + [anywhere] * 3,
        scratch_shapes=scratch,
        compiler_params=pltpu.CompilerParams(
            collective_id=0, has_side_effects=True, vmem_limit_bytes=64 * 1024 * 1024
        ),
        name="feed_forward",
    )(
        positions.reshape(1, BLOCK), segment.reshape(1, BLOCK), log_ratio.reshape(1, BLOCK),
        loaded, token_grad, gate_weight, up_weight, down_weight,
    )
    blocks = [pl.BlockSpec((BLOCK // 2, DB), lambda i: (jnp.minimum(i, 1), 0))] * 2
    blocks += [pl.BlockSpec((o.shape[0] // STEPS, o.shape[1]), lambda i: (i, 0)) for o in outs[2:]]
    return pl.pallas_call(
        hand_over,
        grid=(STEPS,),
        out_shape=tuple(shape(o.shape, o.dtype) for o in outs),
        in_specs=blocks,
        out_specs=blocks,
        compiler_params=pltpu.CompilerParams(vmem_limit_bytes=64 * 1024 * 1024),
        name="hand_over",
    )(*outs)


def solution(mesh):
    return jax.shard_map(
        per_device,
        mesh=mesh,
        in_specs=(
            P("col", "row"),
            P("col"),
            P("row", "col"),
            P("row", "col"),
            P("col", "row"),
            P("col"),
            P("col"),
            P("col", "row"),
        ),
        out_specs=(
            P("col", "row"),
            P("col", "row"),
            P("row", "col"),
            P("row", "col"),
            P("col", "row"),
        ),
        check_vma=False,
    )
```

```python
import jax
import jax.numpy as jnp
from jax import lax
from jax.experimental import pallas as pl
from jax.experimental.pallas import tpu as pltpu
from jax.sharding import PartitionSpec as P

BETA = 0.1
F32, BF16 = jnp.float32, jnp.bfloat16
TOK, DB, FB = 1536, 1024, 896
BLOCK, HALF = 96, 48
CHUNK, SHARE = 384, 48
PLANE = 192
FAR = 384
PLANE_OFF = (2, 1, -1, 0)
MINOR_OFF = (0, 1, -1, 2)
CHUNKS = (
    ((0, 0), (0, 1), (0, 2), (0, 3)),
    ((1, 0), (1, 1), (2, 2), (2, 3)),
    ((2, 0), (2, 1), (1, 2), (1, 3)),
    ((3, 0), (3, 1), (3, 2), (3, 3)),
)
NT = (((0,), (0,)), ((), ()))
TN = (((1,), (1,)), ((), ()))


def rows(start, size):
    return pl.ds(start, size)


def kernel(spots, parts, ratios, loaded, token_grad, gw, uw, dw, mixed, ginp, ggate, gup, gdown, *scratch):
    (tiles, weights, down, xl, xs, grads, pre, pre_pair, pre_r1, pre_r2, pre_share, hid, ghp, gh_pair,
     gh_r1, gh_r2, act, part_m, c1, c2, c3, onehot, onehot_far, places, totals_u, totals_d, small_u, small_s, small_f, held_grad, send, recv, local) = scratch
    part_i = xl
    row, col = lax.axis_index("row"), lax.axis_index("col")
    x, k, z, y = row // 2, row % 2, col // 4, col % 4

    def device(dx=0, dk=0, dz=0, dy=0):
        return {
            "row": lax.rem(x + dx + 4, 4) * 2 + lax.rem(k + dk, 2),
            "col": lax.rem(z + dz + 4, 4) * 4 + lax.rem(y + dy + 4, 4),
        }

    sent, gone = [], set()

    def transfer(src, dst, target, landing=None):
        index = len(sent)
        copy = pltpu.make_async_remote_copy(
            src_ref=src, dst_ref=dst, send_sem=send.at[index], recv_sem=recv.at[index],
            device_id=target, device_id_type=pl.DeviceIdType.MESH,
        )
        copy.start()
        sent.append(copy)
        if landing is None:
            return copy
        return pltpu.make_async_remote_copy(
            src_ref=src, dst_ref=landing, send_sem=send.at[index], recv_sem=recv.at[index],
            device_id=target, device_id_type=pl.DeviceIdType.MESH,
        )

    local_copies = []

    def fetch(src, dst):
        copy = pltpu.make_async_copy(src, dst, local.at[len(local_copies)])
        copy.start()
        local_copies.append(copy)
        return copy

    def along(half, major=0, minor=0):
        return device(dz=major, dy=minor) if half == 0 else device(dz=minor, dy=major)

    def place(half, plane, minor):
        for c, held in enumerate(CHUNKS):
            if (plane, minor) in held:
                return rows(c * CHUNK + half * PLANE + held.index((plane, minor)) * HALF, HALF)

    sources = (spots, parts, ratios, token_grad)
    spots, parts, ratios, token_grad = small_u, small_s, small_f, held_grad
    first_copies = [
        fetch(loaded.at[rows(half * HALF, HALF), :], xl.at[place(half, 3, 0), :]) for half in (0, 1)
    ]
    small_copies = [fetch(a, b) for a, b in zip(sources, (spots, parts, ratios, token_grad))]
    weight_copies = [fetch(gw, weights.at[:, 0:FB]), fetch(uw, weights.at[:, FB : 2 * FB]), fetch(dw, down)]

    others = [(dz, dy) for dz in range(4) for dy in range(4) if (dz, dy) != (0, 0)]
    barrier = pltpu.get_barrier_semaphore()
    peers = [device(dz=dz, dy=dy) for dz, dy in others]
    peers += [device(dx=1), device(dx=-1), device(dk=1)]
    for peer in peers:
        pl.semaphore_signal(barrier, inc=1, device_id=peer, device_id_type=pl.DeviceIdType.MESH)
    pl.semaphore_wait(barrier, len(peers))

    class Gather:
        def __init__(self, buf):
            self.buf, self.got, self.seen, self.left = buf, {}, set(), False

        def move(self, half, src, dst, target):
            self.got[(half,) + dst] = transfer(
                self.buf.at[place(half, *src)], self.buf.at[place(half, *dst)], target
            )

        def spread(self, half, minor):
            self.move(half, (3, minor), (2, minor), along(half, major=1))
            self.move(half, (3, minor), (1, minor), along(half, major=-1))

        def begin(self):
            for half in (0, 1):
                self.move(half, (3, 0), (3, 2), along(half, minor=1))
                self.move(half, (3, 0), (3, 1), along(half, minor=-1))
                self.move(half, (3, 0), (3, 3), along(half, minor=2))
                self.spread(half, 0)

        def wait(self, half, plane, minor):
            if (half, plane, minor) not in self.seen:
                self.got[(half, plane, minor)].wait_recv()
                self.seen.add((half, plane, minor))

        def spread_on(self, half, minor):
            self.wait(half, 3, minor)
            self.spread(half, minor)

        def forward(self, half, minor):
            plane, way = (2, 1) if minor < 2 else (1, -1)
            self.wait(half, plane, minor)
            self.move(half, (plane, minor), (0, minor), along(half, major=way))

        def need(self, *chunks):
            for c in chunks:
                for half in (0, 1):
                    for plane, minor in CHUNKS[c]:
                        if (plane, minor) != (3, 0):
                            self.wait(half, plane, minor)

    gather_x, gather_g = Gather(xl), Gather(grads)
    for copy in first_copies:
        copy.wait()
    tile_copies = []

    def send_tiles():
        for copy in small_copies:
            copy.wait()
        tiles[0:8, :] = jnp.full((8, 128), -1.0, F32)
        tiles[0:1, 0:BLOCK] = spots[...].astype(F32)
        tiles[1:2, 0:BLOCK] = parts[...].astype(F32)
        tiles[2:3, 0:BLOCK] = ratios[...]
        for dz, dy in others:
            slot = ((-dz) % 4) * 4 + (-dy) % 4
            tile_copies.append(
                transfer(tiles.at[0:8, :], tiles.at[slot * 8 : slot * 8 + 8, :], device(dz=dz, dy=dy))
            )

    def slot_of(half, plane, minor):
        major, less = PLANE_OFF[plane] % 4, MINOR_OFF[minor] % 4
        return major * 4 + less if half == 0 else less * 4 + major

    def tables():
        for copy in tile_copies:
            copy.wait_recv()
        table = tiles[...]
        turned = table.T
        for half in (0, 1):
            for plane in range(4):
                for minor in range(4):
                    lane = slot_of(half, plane, minor) * 8
                    column = turned[half * HALF : half * HALF + HALF, lane : lane + 1]
                    places[place(half, plane, minor), :] = jnp.broadcast_to(column, (HALF, 128)).astype(jnp.int32)
        segment_part = jnp.concatenate([table[8 * i + 1 : 8 * i + 2, :] for i in range(16)], 0)
        ratio_part = jnp.concatenate([table[8 * i + 2 : 8 * i + 3, :] for i in range(16)], 0)

        def total(s):
            return jnp.sum(jnp.where(segment_part == float(s), ratio_part, 0.0), axis=(0, 1), keepdims=True)

        own_segment = turned[0:BLOCK, 1:2]
        token_weight = jnp.zeros((BLOCK, 1), F32)
        for p in range(4):
            margin = BETA * (total(2 * p) - total(2 * p + 1))
            pair_weight = -BETA * jax.nn.sigmoid(-margin)
            token_weight = jnp.where(own_segment == float(2 * p), pair_weight, token_weight)
            token_weight = jnp.where(own_segment == float(2 * p + 1), -pair_weight, token_weight)
        for half in (0, 1):
            part = rows(half * HALF, HALF)
            weight = token_weight[half * HALF : half * HALF + HALF, :]
            grads[place(half, 3, 0), :] = (weight * token_grad[part, :].astype(F32)).astype(BF16)

    ready = []

    def need_weights():
        if not ready:
            for copy in weight_copies:
                copy.wait()
            ready.append(True)

    def tokens_of(c):
        lane = lax.broadcasted_iota(jnp.int32, (1, CHUNK), 1)
        token = lane
        for j in range(8):
            half, (plane, minor) = j // 4, CHUNKS[c][j % 4]
            major, less = PLANE_OFF[plane], MINOR_OFF[minor]
            dz, dy = (major, less) if half == 0 else (less, major)
            block = lax.rem(z + dz + 4, 4) * 4 + lax.rem(y + dy + 4, 4)
            inside = (lane >= j * HALF) & (lane < (j + 1) * HALF)
            token = token + jnp.where(inside, block * BLOCK + half * HALF - j * HALF, 0)
        return token

    def match(c, first, count, ref):
        token = tokens_of(c)

        def build(i, carry):
            part = rows(pl.multiple_of(i * 128, 128), 128)
            here = places[rows(pl.multiple_of(first + i * 128, 128), 128), :]
            for j in range(0, CHUNK, 128):
                ref[part, j : j + 128] = jnp.where(here == token[:, j : j + 128], 1.0, 0.0).astype(BF16)
            return carry

        lax.fori_loop(0, count // 128, build, 0)

    def permute_most(c):
        gather_x.need(1, 2, 3)
        match(c, FAR, TOK - FAR, onehot)
        xs[rows(c * CHUNK, CHUNK), :] = lax.dot_general(
            onehot[...], xl[FAR:TOK, :], NT, preferred_element_type=F32
        ).astype(BF16)

    def permute_rest(c):
        gather_x.need(0)
        match(c, 0, FAR, onehot_far)
        chunk = rows(c * CHUNK, CHUNK)
        rest = lax.dot_general(onehot_far[...], xl[0:FAR, :], NT, preferred_element_type=F32)
        xs[chunk, :] = (xs[chunk, :].astype(F32) + rest).astype(BF16)

    def pre_matmul(c, i):
        need_weights()
        chunk, cols = rows(c * CHUNK, CHUNK), rows(i * FB, FB)
        pre[chunk, cols] = jnp.dot(xs[chunk, :], weights[:, cols], preferred_element_type=F32).astype(BF16)
        forward[c].pair_send(i)

    def gh_matmul(c):
        need_weights()
        gather_g.need(c)
        chunk = rows(c * CHUNK, CHUNK)
        ghp[chunk, :] = lax.dot_general(grads[chunk, :], down[...], TN, preferred_element_type=F32).astype(BF16)
        backward[c].pair_send(0)

    def mixed_matmul(c):
        chunk = rows(c * CHUNK, CHUNK)
        forward[c].out_wait()
        part_m[chunk, :] = jnp.dot(hid[chunk, :], down[...], preferred_element_type=F32).astype(BF16)

    def ginp_matmul(c):
        chunk = rows(c * CHUNK, CHUNK)
        backward[c].out_wait()
        if not gather_x.left:
            gather_x.left = True
            for copy in gather_x.got.values():
                copy.wait_send()
                gone.add(id(copy))
        part_i[chunk, :] = lax.dot_general(
            act[chunk, :], weights[...], TN, preferred_element_type=F32
        ).astype(BF16)

    xp, xm, xo = lax.rem(x + 1, 4), lax.rem(x + 3, 4), lax.rem(x + 2, 4)

    class RowChunk:
        def __init__(self, c, part, pair, r1, r2, width, out, out_width):
            self.c, self.part, self.pair, self.r1, self.r2 = c, part, pair, r1, r2
            self.width, self.out, self.out_width = width, out, out_width
            self.pairs, self.far, self.near, self.last = {}, {}, {}, {}

        def cut(self, width):
            if width == 2 * FB:
                return FB
            return 512 if self.c % 2 == 0 else 384

        def mine(self, xx):
            return rows(pl.multiple_of(self.c * CHUNK + k * PLANE + xx * SHARE, 16), SHARE)

        def pair_send(self, i):
            theirs = rows(pl.multiple_of(self.c * CHUNK + (1 - k) * PLANE, 16), PLANE)
            cols = rows(i * FB, FB)
            self.pairs[i] = transfer(self.part.at[theirs, cols], self.pair.at[self.c, :, cols], device(dk=1))

        def pair_add(self, i):
            self.pairs[i].wait_recv()
            mine, cols = rows(pl.multiple_of(self.c * CHUNK + k * PLANE, 16), PLANE), rows(i * FB, FB)
            both = self.part[mine, cols].astype(F32) + self.pair[self.c, :, cols].astype(F32)
            self.part[mine, cols] = both.astype(BF16)
            cut, far = self.cut(self.width), self.mine(xo)
            for way, lo, hi, dx in ((0, 0, cut, 1), (1, cut, self.width, -1)):
                if self.width == FB or way == i:
                    self.far[way] = transfer(
                        self.part.at[far, lo:hi], self.r1.at[self.c, :, lo:hi], device(dx=dx)
                    )

        def ring_add(self, i):
            cut = self.cut(self.width)
            xx, lo, hi, dx = ((xp, 0, cut, 1), (xm, cut, self.width, -1))[i]
            self.far[i].wait_recv()
            mine = self.mine(xx)
            both = self.part[mine, lo:hi].astype(F32) + self.r1[self.c, :, lo:hi].astype(F32)
            self.part[mine, lo:hi] = both.astype(BF16)
            self.near[i] = transfer(self.part.at[mine, :], self.r2.at[self.c, i], device(dx=dx))

        def total(self):
            self.near[0].wait_recv()
            self.near[1].wait_recv()
            return (
                self.part[self.mine(x), :].astype(F32)
                + self.r2[self.c, 0].astype(F32)
                + self.r2[self.c, 1].astype(F32)
            )

        def out_send(self):
            own = self.out.at[self.mine(x), :]
            self.side = [
                transfer(own, own, device(dx=1), self.out.at[self.mine(xm), :]),
                transfer(own, own, device(dx=-1), self.out.at[self.mine(xp), :]),
            ]
            self.done = []
            self.over(x)

        def over(self, xx):
            mine = self.out.at[self.mine(xx), :]
            other = rows(pl.multiple_of(self.c * CHUNK + (1 - k) * PLANE + xx * SHARE, 16), SHARE)
            self.done.append(transfer(mine, mine, device(dk=1), self.out.at[other, :]))

        def out_forward(self, i):
            cut = self.cut(self.out_width)
            xx, lo, hi, dx = ((xm, 0, cut, 1), (xp, cut, self.out_width, -1))[i]
            self.side[i].wait_recv()
            piece = self.out.at[self.mine(xx), lo:hi]
            self.last[i] = transfer(piece, piece, device(dx=dx), self.out.at[self.mine(xo), lo:hi])
            self.over(xx)

        def out_pair(self):
            self.last[0].wait_recv()
            self.last[1].wait_recv()
            self.over(xo)

        def out_wait(self):
            for copy in self.done:
                copy.wait_recv()
            self.done = []

    forward = [RowChunk(c, pre, pre_pair, pre_r1, pre_r2, 2 * FB, hid, FB) for c in range(4)]
    backward = [RowChunk(c, ghp, gh_pair, gh_r1, gh_r2, FB, act, 2 * FB) for c in range(4)]

    def hidden(c):
        both = forward[c].total()
        pre_share[c] = both
        gate, up = both[:, :FB], both[:, FB:]
        hid[forward[c].mine(x), :] = (gate * jax.nn.sigmoid(gate) * up).astype(BF16)
        forward[c].out_send()

    def acts(c):
        grad = backward[c].total()
        gate, up = pre_share[c, :, 0:FB], pre_share[c, :, FB : 2 * FB]
        s = jax.nn.sigmoid(gate)
        mine = backward[c].mine(x)
        act[mine, 0:FB] = (grad * up * s * (1.0 + gate * (1.0 - s))).astype(BF16)
        act[mine, FB : 2 * FB] = (grad * gate * s).astype(BF16)
        backward[c].out_send()

    class ColSum:
        def __init__(self, half, which, part, out):
            self.half, self.part, self.out = half, part, out
            self.c1, self.c2, self.c3 = c1.at[which], c2.at[which], c3.at[which]

        def part_of(self, c, i):
            return rows(c * CHUNK + self.half * PLANE + i * 96, 96)

        def near_send(self, c, i, way):
            to = 0 if way == 1 else 1
            self.near.append(
                transfer(
                    self.part.at[self.part_of(c, i), :],
                    self.c2.at[to, i * 96 : i * 96 + 96, :],
                    along(self.half, major=way),
                )
            )

        def send_far(self):
            self.far = [
                transfer(self.part.at[self.part_of(0, i), :], self.c1.at[i], along(self.half, major=1 - 2 * i))
                for i in (0, 1)
            ]
            self.near = []

        def send_near(self, i):
            self.far[i].wait_recv()
            mine = self.part_of(1, i)
            self.part[mine, :] = (self.part[mine, :].astype(F32) + self.c1[i].astype(F32)).astype(BF16)
            self.near_send(1, i, 1 - 2 * i)

        def send_rest(self):
            self.near_send(2, 0, -1)
            self.near_send(2, 1, 1)

        def send_minor(self):
            for copy in self.near:
                copy.wait_recv()
            start = 3 * CHUNK + self.half * PLANE
            own = rows(start, PLANE)
            self.part[own, :] = (
                self.part[own, :].astype(F32) + self.c2[0].astype(F32) + self.c2[1].astype(F32)
            ).astype(BF16)
            self.minor = [
                transfer(
                    self.part.at[rows(start + m * HALF, HALF), :],
                    self.c3.at[m - 1],
                    along(self.half, minor=MINOR_OFF[m]),
                )
                for m in (1, 2, 3)
            ]

        def store(self):
            total = self.part[rows(3 * CHUNK + self.half * PLANE, HALF), :].astype(F32)
            for i in range(3):
                self.minor[i].wait_recv()
                total = total + self.c3[i].astype(F32)
            self.out[rows(self.half * HALF, HALF), :] = total.astype(BF16)

    mixed_sum = [ColSum(h, h, part_m, mixed) for h in (0, 1)]
    ginp_sum = [ColSum(h, 2 + h, part_i, ginp) for h in (0, 1)]

    stores = []

    def tile(i):
        return rows(pl.multiple_of(i * 256, 256), 256)

    def keep(which, i, src, dst):
        copy = pltpu.make_async_copy(src, dst, local.at[16 + which * 4 + i])
        copy.start()
        return copy

    def down_grad(first):
        part = rows(first * CHUNK, 2 * CHUNK)
        gather_g.need(first, first + 1)
        for c in (first, first + 1):
            forward[c].out_wait()

        def body(i, carry):
            new = lax.dot_general(hid[part, :], grads[part, tile(i)], NT, preferred_element_type=F32)
            totals_d[i] = totals_d[i] + new if first else new
            if first:
                keep(2, i, totals_d.at[i], gdown.at[:, tile(i)])
            return carry

        lax.fori_loop(0, 4, body, 0)
        if first:
            for i in range(4):
                stores.append((2, i, totals_d.at[i], gdown.at[:, rows(i * 256, 256)]))

    def up_grad(which, first):
        part, wide = rows(first * CHUNK, 2 * CHUNK), rows(which * FB, FB)
        target = (ggate, gup)[which]
        for c in (first, first + 1):
            backward[c].out_wait()

        def body(i, carry):
            new = lax.dot_general(xs[part, tile(i)], act[part, wide], NT, preferred_element_type=F32)
            totals_u[tile(i), wide] = totals_u[tile(i), wide] + new if first else new
            if first:
                keep(which, i, totals_u.at[tile(i), wide], target.at[tile(i), :])
            return carry

        lax.fori_loop(0, 4, body, 0)
        if first:
            for i in range(4):
                cols = rows(i * 256, 256)
                stores.append((which, i, totals_u.at[cols, wide], target.at[cols, :]))

    gather_x.begin()
    send_tiles()
    gather_x.spread_on(0, 2)
    gather_x.forward(0, 0)
    gather_x.spread_on(0, 1)
    gather_x.spread_on(0, 3)
    gather_x.spread_on(1, 2)
    gather_x.spread_on(1, 1)
    gather_x.spread_on(1, 3)
    gather_x.forward(1, 0)
    tables()
    gather_x.forward(0, 2)
    gather_x.forward(1, 2)
    gather_x.forward(1, 1)
    gather_x.forward(1, 3)
    gather_x.forward(0, 3)
    gather_x.forward(0, 1)
    gather_g.begin()
    permute_most(2)
    permute_most(0)
    permute_rest(0)
    pre_matmul(0, 0)
    gather_g.spread_on(0, 1)
    pre_matmul(0, 1)
    permute_rest(2)
    gather_g.spread_on(0, 3)
    gather_g.spread_on(1, 1)
    pre_matmul(2, 0)
    pre_matmul(2, 1)
    gather_g.spread_on(1, 3)
    gather_g.spread_on(0, 2)
    forward[0].pair_add(0)
    forward[2].pair_add(0)
    forward[0].pair_add(1)
    gather_g.forward(0, 0)
    gather_g.forward(0, 1)
    forward[2].pair_add(1)
    gather_g.forward(1, 0)
    gather_g.forward(1, 1)
    gather_g.spread_on(1, 2)
    permute_most(1)
    permute_rest(1)
    forward[0].ring_add(0)
    forward[0].ring_add(1)
    gather_g.forward(1, 3)
    gather_g.forward(0, 3)
    pre_matmul(1, 0)
    forward[2].ring_add(0)
    gather_g.forward(0, 2)
    forward[2].ring_add(1)
    pre_matmul(1, 1)
    forward[1].pair_add(0)
    gather_g.forward(1, 2)
    gh_matmul(2)
    gh_matmul(3)
    forward[1].pair_add(1)
    hidden(0)
    backward[2].pair_add(0)
    gh_matmul(1)
    backward[3].pair_add(0)
    gh_matmul(0)
    permute_most(3)
    backward[0].pair_add(0)
    backward[1].pair_add(0)
    forward[1].ring_add(0)
    forward[1].ring_add(1)
    hidden(2)
    permute_rest(3)
    pre_matmul(3, 0)
    backward[2].ring_add(0)
    backward[2].ring_add(1)
    forward[0].out_forward(0)
    forward[0].out_forward(1)
    pre_matmul(3, 1)
    forward[3].pair_add(0)
    backward[3].ring_add(1)
    backward[3].ring_add(0)
    backward[0].ring_add(0)
    backward[0].ring_add(1)
    backward[1].ring_add(0)
    backward[1].ring_add(1)
    forward[3].pair_add(1)
    hidden(1)
    forward[2].out_forward(0)
    forward[2].out_forward(1)
    acts(2)
    forward[0].out_pair()
    mixed_matmul(0)
    forward[3].ring_add(0)
    mixed_sum[0].send_far()
    mixed_sum[1].send_far()
    acts(0)
    acts(1)
    forward[3].ring_add(1)
    forward[1].out_forward(0)
    forward[1].out_forward(1)
    forward[2].out_pair()
    mixed_matmul(2)
    mixed_sum[1].send_rest()
    mixed_sum[0].send_rest()
    backward[2].out_forward(0)
    backward[2].out_forward(1)
    backward[0].out_forward(1)
    backward[0].out_forward(0)
    backward[1].out_forward(1)
    backward[1].out_forward(0)
    hidden(3)
    acts(3)
    forward[1].out_pair()
    mixed_matmul(1)
    mixed_sum[0].send_near(0)
    backward[2].out_pair()
    mixed_sum[1].send_near(0)
    mixed_sum[1].send_near(1)
    mixed_sum[0].send_near(1)
    down_grad(0)
    backward[0].out_pair()
    ginp_matmul(2)
    backward[1].out_pair()
    ginp_matmul(0)
    ginp_sum[1].send_far()
    ginp_sum[0].send_far()
    ginp_matmul(1)
    ginp_sum[0].send_rest()
    forward[3].out_forward(0)
    forward[3].out_forward(1)
    ginp_sum[1].send_rest()
    up_grad(0, 0)
    backward[3].out_forward(1)
    ginp_sum[1].send_near(1)
    ginp_sum[0].send_near(1)
    ginp_sum[1].send_near(0)
    ginp_sum[0].send_near(0)
    forward[3].out_pair()
    backward[3].out_forward(0)
    up_grad(1, 0)
    mixed_matmul(3)
    down_grad(2)
    mixed_sum[0].send_minor()
    backward[3].out_pair()
    mixed_sum[1].send_minor()
    ginp_matmul(3)
    ginp_sum[0].send_minor()
    ginp_sum[1].send_minor()
    up_grad(0, 2)
    mixed_sum[1].store()
    mixed_sum[0].store()
    up_grad(1, 2)
    ginp_sum[1].store()
    ginp_sum[0].store()
    for which, i, src, dst in stores:
        pltpu.make_async_copy(src, dst, local.at[16 + which * 4 + i]).wait()
    for copy in sent:
        if id(copy) not in gone:
            copy.wait_send()


STEPS = 4


def hand_over(*refs):
    for src, dst in zip(refs[:5], refs[5:]):
        dst[...] = src[...]


def per_device(loaded, positions, gate_weight, up_weight, down_weight, segment, log_ratio, token_grad):
    vmem, anywhere = pl.BlockSpec(memory_space=pltpu.VMEM), pl.BlockSpec(memory_space=pl.ANY)
    shape = jax.ShapeDtypeStruct
    buf = lambda *s: pltpu.VMEM(s, BF16)
    transfers = 220
    scratch = [
        pltpu.VMEM((128, 128), F32),
        buf(DB, 2 * FB),
        buf(FB, DB),
        buf(TOK, DB),
        buf(TOK, DB),
        buf(TOK, DB),
        buf(TOK, 2 * FB),
        buf(4, PLANE, 2 * FB),
        buf(4, SHARE, 2 * FB),
        buf(4, 2, SHARE, 2 * FB),
        pltpu.VMEM((4, SHARE, 2 * FB), F32),
        buf(TOK, FB),
        buf(TOK, FB),
        buf(4, PLANE, FB),
        buf(4, SHARE, FB),
        buf(4, 2, SHARE, FB),
        buf(TOK, 2 * FB),
        buf(TOK, DB),
        buf(4, 2, 96, DB),
        buf(4, 2, PLANE, DB),
        buf(4, 3, HALF, DB),
        buf(TOK - FAR, CHUNK),
        buf(FAR, CHUNK),
        pltpu.VMEM((TOK, 128), jnp.int32),
        pltpu.VMEM((DB, 2 * FB), F32),
        pltpu.VMEM((4, FB, 256), F32),
        pltpu.VMEM((1, BLOCK), jnp.int32),
        pltpu.VMEM((1, BLOCK), jnp.int32),
        pltpu.VMEM((1, BLOCK), F32),
        buf(BLOCK, DB),
        pltpu.SemaphoreType.DMA((transfers,)),
        pltpu.SemaphoreType.DMA((transfers,)),
        pltpu.SemaphoreType.DMA((32,)),
    ]
    outs = pl.pallas_call(
        kernel,
        out_shape=(
            shape((BLOCK, DB), BF16),
            shape((BLOCK, DB), BF16),
            shape((DB, FB), F32),
            shape((DB, FB), F32),
            shape((FB, DB), F32),
        ),
        in_specs=[anywhere] * 8,
        out_specs=[vmem] * 2 + [anywhere] * 3,
        scratch_shapes=scratch,
        compiler_params=pltpu.CompilerParams(
            collective_id=0, has_side_effects=True, vmem_limit_bytes=64 * 1024 * 1024
        ),
        name="feed_forward",
    )(
        positions.reshape(1, BLOCK), segment.reshape(1, BLOCK), log_ratio.reshape(1, BLOCK),
        loaded, token_grad, gate_weight, up_weight, down_weight,
    )
    blocks = [pl.BlockSpec((BLOCK // 2, DB), lambda i: (jnp.minimum(i, 1), 0))] * 2
    blocks += [pl.BlockSpec((o.shape[0] // STEPS, o.shape[1]), lambda i: (i, 0)) for o in outs[2:]]
    return pl.pallas_call(
        hand_over,
        grid=(STEPS,),
        out_shape=tuple(shape(o.shape, o.dtype) for o in outs),
        in_specs=blocks,
        out_specs=blocks,
        compiler_params=pltpu.CompilerParams(vmem_limit_bytes=64 * 1024 * 1024),
        name="hand_over",
    )(*outs)


def solution(mesh):
    return jax.shard_map(
        per_device,
        mesh=mesh,
        in_specs=(
            P("col", "row"),
            P("col"),
            P("row", "col"),
            P("row", "col"),
            P("col", "row"),
            P("col"),
            P("col"),
            P("col", "row"),
        ),
        out_specs=(
            P("col", "row"),
            P("col", "row"),
            P("row", "col"),
            P("row", "col"),
            P("col", "row"),
        ),
        check_vma=False,
    )
```

```python
import jax
import jax.numpy as jnp
from jax import lax
from jax.experimental import pallas as pl
from jax.experimental.pallas import tpu as pltpu
from jax.sharding import PartitionSpec as P

BETA = 0.1
F32, BF16 = jnp.float32, jnp.bfloat16
TOK, DB, FB = 1536, 1024, 896
BLOCK, HALF = 96, 48
CHUNK, SHARE = 384, 48
PLANE = 192
FAR = 384
PLANE_OFF = (2, 1, -1, 0)
MINOR_OFF = (0, 1, -1, 2)
CHUNKS = (
    ((0, 0), (0, 1), (0, 2), (0, 3)),
    ((1, 0), (1, 1), (2, 2), (2, 3)),
    ((2, 0), (2, 1), (1, 2), (1, 3)),
    ((3, 0), (3, 1), (3, 2), (3, 3)),
)
NT = (((0,), (0,)), ((), ()))
TN = (((1,), (1,)), ((), ()))


def rows(start, size):
    return pl.ds(start, size)


def kernel(spots, parts, ratios, loaded, token_grad, gw, uw, dw, mixed, ginp, ggate, gup, gdown, *scratch):
    (tiles, weights, down, xl, xs, grads, pre, pre_pair, pre_r1, pre_r2, pre_share, hid, ghp, gh_pair,
     gh_r1, gh_r2, act, part_m, c1, c2, c3, onehot, onehot_far, places, totals_u, totals_d, small_u, small_s, small_f, held_grad, send, recv, local) = scratch
    part_i = xl
    row, col = lax.axis_index("row"), lax.axis_index("col")
    x, k, z, y = row // 2, row % 2, col // 4, col % 4

    def device(dx=0, dk=0, dz=0, dy=0):
        return {
            "row": lax.rem(x + dx + 4, 4) * 2 + lax.rem(k + dk, 2),
            "col": lax.rem(z + dz + 4, 4) * 4 + lax.rem(y + dy + 4, 4),
        }

    sent, gone = [], set()

    def transfer(src, dst, target, landing=None):
        index = len(sent)
        copy = pltpu.make_async_remote_copy(
            src_ref=src, dst_ref=dst, send_sem=send.at[index], recv_sem=recv.at[index],
            device_id=target, device_id_type=pl.DeviceIdType.MESH,
        )
        copy.start()
        sent.append(copy)
        if landing is None:
            return copy
        return pltpu.make_async_remote_copy(
            src_ref=src, dst_ref=landing, send_sem=send.at[index], recv_sem=recv.at[index],
            device_id=target, device_id_type=pl.DeviceIdType.MESH,
        )

    local_copies = []

    def fetch(src, dst):
        copy = pltpu.make_async_copy(src, dst, local.at[len(local_copies)])
        copy.start()
        local_copies.append(copy)
        return copy

    def along(half, major=0, minor=0):
        return device(dz=major, dy=minor) if half == 0 else device(dz=minor, dy=major)

    def place(half, plane, minor):
        for c, held in enumerate(CHUNKS):
            if (plane, minor) in held:
                return rows(c * CHUNK + half * PLANE + held.index((plane, minor)) * HALF, HALF)

    sources = (spots, parts, ratios, token_grad)
    spots, parts, ratios, token_grad = small_u, small_s, small_f, held_grad
    first_copies = [
        fetch(loaded.at[rows(half * HALF, HALF), :], xl.at[place(half, 3, 0), :]) for half in (0, 1)
    ]
    small_copies = [fetch(a, b) for a, b in zip(sources, (spots, parts, ratios, token_grad))]
    weight_copies = [fetch(gw, weights.at[:, 0:FB]), fetch(uw, weights.at[:, FB : 2 * FB]), fetch(dw, down)]

    others = [(dz, dy) for dz in range(4) for dy in range(4) if (dz, dy) != (0, 0)]
    barrier = pltpu.get_barrier_semaphore()
    peers = [device(dz=dz, dy=dy) for dz, dy in others]
    peers += [device(dx=1), device(dx=-1), device(dk=1)]
    for peer in peers:
        pl.semaphore_signal(barrier, inc=1, device_id=peer, device_id_type=pl.DeviceIdType.MESH)
    pl.semaphore_wait(barrier, len(peers))

    class Gather:
        def __init__(self, buf):
            self.buf, self.got, self.seen, self.left = buf, {}, set(), False

        def move(self, half, src, dst, target):
            self.got[(half,) + dst] = transfer(
                self.buf.at[place(half, *src)], self.buf.at[place(half, *dst)], target
            )

        def spread(self, half, minor):
            self.move(half, (3, minor), (2, minor), along(half, major=1))
            self.move(half, (3, minor), (1, minor), along(half, major=-1))

        def begin(self):
            for half in (0, 1):
                self.move(half, (3, 0), (3, 2), along(half, minor=1))
                self.move(half, (3, 0), (3, 1), along(half, minor=-1))
                self.move(half, (3, 0), (3, 3), along(half, minor=2))
                self.spread(half, 0)

        def wait(self, half, plane, minor):
            if (half, plane, minor) not in self.seen:
                self.got[(half, plane, minor)].wait_recv()
                self.seen.add((half, plane, minor))

        def spread_on(self, half, minor):
            self.wait(half, 3, minor)
            self.spread(half, minor)

        def forward(self, half, minor):
            plane, way = (2, 1) if minor < 2 else (1, -1)
            self.wait(half, plane, minor)
            self.move(half, (plane, minor), (0, minor), along(half, major=way))

        def need(self, *chunks):
            for c in chunks:
                for half in (0, 1):
                    for plane, minor in CHUNKS[c]:
                        if (plane, minor) != (3, 0):
                            self.wait(half, plane, minor)

    gather_x, gather_g = Gather(xl), Gather(grads)
    for copy in first_copies:
        copy.wait()
    tile_copies = []

    def send_tiles():
        for copy in small_copies:
            copy.wait()
        tiles[0:8, :] = jnp.full((8, 128), -1.0, F32)
        tiles[0:1, 0:BLOCK] = spots[...].astype(F32)
        tiles[1:2, 0:BLOCK] = parts[...].astype(F32)
        tiles[2:3, 0:BLOCK] = ratios[...]
        for dz, dy in others:
            slot = ((-dz) % 4) * 4 + (-dy) % 4
            tile_copies.append(
                transfer(tiles.at[0:8, :], tiles.at[slot * 8 : slot * 8 + 8, :], device(dz=dz, dy=dy))
            )

    def slot_of(half, plane, minor):
        major, less = PLANE_OFF[plane] % 4, MINOR_OFF[minor] % 4
        return major * 4 + less if half == 0 else less * 4 + major

    def tables():
        for copy in tile_copies:
            copy.wait_recv()
        table = tiles[...]
        turned = table.T
        for half in (0, 1):
            for plane in range(4):
                for minor in range(4):
                    lane = slot_of(half, plane, minor) * 8
                    column = turned[half * HALF : half * HALF + HALF, lane : lane + 1]
                    places[place(half, plane, minor), :] = jnp.broadcast_to(column, (HALF, 128)).astype(jnp.int32)
        segment_part = jnp.concatenate([table[8 * i + 1 : 8 * i + 2, :] for i in range(16)], 0)
        ratio_part = jnp.concatenate([table[8 * i + 2 : 8 * i + 3, :] for i in range(16)], 0)

        def total(s):
            return jnp.sum(jnp.where(segment_part == float(s), ratio_part, 0.0), axis=(0, 1), keepdims=True)

        own_segment = turned[0:BLOCK, 1:2]
        token_weight = jnp.zeros((BLOCK, 1), F32)
        for p in range(4):
            margin = BETA * (total(2 * p) - total(2 * p + 1))
            pair_weight = -BETA * jax.nn.sigmoid(-margin)
            token_weight = jnp.where(own_segment == float(2 * p), pair_weight, token_weight)
            token_weight = jnp.where(own_segment == float(2 * p + 1), -pair_weight, token_weight)
        for half in (0, 1):
            part = rows(half * HALF, HALF)
            weight = token_weight[half * HALF : half * HALF + HALF, :]
            grads[place(half, 3, 0), :] = (weight * token_grad[part, :].astype(F32)).astype(BF16)

    ready = []

    def need_weights():
        if not ready:
            for copy in weight_copies:
                copy.wait()
            ready.append(True)

    def tokens_of(c):
        lane = lax.broadcasted_iota(jnp.int32, (1, CHUNK), 1)
        token = lane
        for j in range(8):
            half, (plane, minor) = j // 4, CHUNKS[c][j % 4]
            major, less = PLANE_OFF[plane], MINOR_OFF[minor]
            dz, dy = (major, less) if half == 0 else (less, major)
            block = lax.rem(z + dz + 4, 4) * 4 + lax.rem(y + dy + 4, 4)
            inside = (lane >= j * HALF) & (lane < (j + 1) * HALF)
            token = token + jnp.where(inside, block * BLOCK + half * HALF - j * HALF, 0)
        return token

    def match(c, first, count, ref):
        token = tokens_of(c)

        def build(i, carry):
            part = rows(pl.multiple_of(i * 128, 128), 128)
            here = places[rows(pl.multiple_of(first + i * 128, 128), 128), :]
            for j in range(0, CHUNK, 128):
                ref[part, j : j + 128] = jnp.where(here == token[:, j : j + 128], 1.0, 0.0).astype(BF16)
            return carry

        lax.fori_loop(0, count // 128, build, 0)

    def permute_most(c):
        gather_x.need(1, 2, 3)
        match(c, FAR, TOK - FAR, onehot)
        xs[rows(c * CHUNK, CHUNK), :] = lax.dot_general(
            onehot[...], xl[FAR:TOK, :], NT, preferred_element_type=F32
        ).astype(BF16)

    def permute_rest(c):
        gather_x.need(0)
        match(c, 0, FAR, onehot_far)
        chunk = rows(c * CHUNK, CHUNK)
        rest = lax.dot_general(onehot_far[...], xl[0:FAR, :], NT, preferred_element_type=F32)
        xs[chunk, :] = (xs[chunk, :].astype(F32) + rest).astype(BF16)

    def pre_matmul(c, i):
        need_weights()
        chunk, cols = rows(c * CHUNK, CHUNK), rows(i * FB, FB)
        pre[chunk, cols] = jnp.dot(xs[chunk, :], weights[:, cols], preferred_element_type=F32).astype(BF16)
        forward[c].pair_send(i)

    def gh_matmul(c):
        need_weights()
        gather_g.need(c)
        chunk = rows(c * CHUNK, CHUNK)
        ghp[chunk, :] = lax.dot_general(grads[chunk, :], down[...], TN, preferred_element_type=F32).astype(BF16)
        backward[c].pair_send(0)

    def mixed_matmul(c):
        chunk = rows(c * CHUNK, CHUNK)
        forward[c].out_wait()
        part_m[chunk, :] = jnp.dot(hid[chunk, :], down[...], preferred_element_type=F32).astype(BF16)

    def ginp_matmul(c):
        chunk = rows(c * CHUNK, CHUNK)
        backward[c].out_wait()
        if not gather_x.left:
            gather_x.left = True
            for copy in gather_x.got.values():
                copy.wait_send()
                gone.add(id(copy))
        part_i[chunk, :] = lax.dot_general(
            act[chunk, :], weights[...], TN, preferred_element_type=F32
        ).astype(BF16)

    xp, xm, xo = lax.rem(x + 1, 4), lax.rem(x + 3, 4), lax.rem(x + 2, 4)

    class RowChunk:
        def __init__(self, c, part, pair, r1, r2, width, out, out_width):
            self.c, self.part, self.pair, self.r1, self.r2 = c, part, pair, r1, r2
            self.width, self.out, self.out_width = width, out, out_width
            self.pairs, self.far, self.near, self.last = {}, {}, {}, {}

        def cut(self, width):
            if width == 2 * FB:
                return FB
            return 512 if self.c % 2 == 0 else 384

        def mine(self, xx):
            return rows(pl.multiple_of(self.c * CHUNK + k * PLANE + xx * SHARE, 16), SHARE)

        def pair_send(self, i):
            theirs = rows(pl.multiple_of(self.c * CHUNK + (1 - k) * PLANE, 16), PLANE)
            cols = rows(i * FB, FB)
            self.pairs[i] = transfer(self.part.at[theirs, cols], self.pair.at[self.c, :, cols], device(dk=1))

        def pair_add(self, i):
            self.pairs[i].wait_recv()
            mine, cols = rows(pl.multiple_of(self.c * CHUNK + k * PLANE, 16), PLANE), rows(i * FB, FB)
            both = self.part[mine, cols].astype(F32) + self.pair[self.c, :, cols].astype(F32)
            self.part[mine, cols] = both.astype(BF16)
            cut, far = self.cut(self.width), self.mine(xo)
            for way, lo, hi, dx in ((0, 0, cut, 1), (1, cut, self.width, -1)):
                if self.width == FB or way == i:
                    self.far[way] = transfer(
                        self.part.at[far, lo:hi], self.r1.at[self.c, :, lo:hi], device(dx=dx)
                    )

        def ring_add(self, i):
            cut = self.cut(self.width)
            xx, lo, hi, dx = ((xp, 0, cut, 1), (xm, cut, self.width, -1))[i]
            self.far[i].wait_recv()
            mine = self.mine(xx)
            both = self.part[mine, lo:hi].astype(F32) + self.r1[self.c, :, lo:hi].astype(F32)
            self.part[mine, lo:hi] = both.astype(BF16)
            self.near[i] = transfer(self.part.at[mine, :], self.r2.at[self.c, i], device(dx=dx))

        def total(self):
            self.near[0].wait_recv()
            self.near[1].wait_recv()
            return (
                self.part[self.mine(x), :].astype(F32)
                + self.r2[self.c, 0].astype(F32)
                + self.r2[self.c, 1].astype(F32)
            )

        def out_send(self):
            own = self.out.at[self.mine(x), :]
            self.side = [
                transfer(own, own, device(dx=1), self.out.at[self.mine(xm), :]),
                transfer(own, own, device(dx=-1), self.out.at[self.mine(xp), :]),
            ]
            self.done = []
            self.over(x)

        def over(self, xx):
            mine = self.out.at[self.mine(xx), :]
            other = rows(pl.multiple_of(self.c * CHUNK + (1 - k) * PLANE + xx * SHARE, 16), SHARE)
            self.done.append(transfer(mine, mine, device(dk=1), self.out.at[other, :]))

        def out_forward(self, i):
            cut = self.cut(self.out_width)
            xx, lo, hi, dx = ((xm, 0, cut, 1), (xp, cut, self.out_width, -1))[i]
            self.side[i].wait_recv()
            piece = self.out.at[self.mine(xx), lo:hi]
            self.last[i] = transfer(piece, piece, device(dx=dx), self.out.at[self.mine(xo), lo:hi])
            self.over(xx)

        def out_pair(self):
            self.last[0].wait_recv()
            self.last[1].wait_recv()
            self.over(xo)

        def out_wait(self):
            for copy in self.done:
                copy.wait_recv()
            self.done = []

    forward = [RowChunk(c, pre, pre_pair, pre_r1, pre_r2, 2 * FB, hid, FB) for c in range(4)]
    backward = [RowChunk(c, ghp, gh_pair, gh_r1, gh_r2, FB, act, 2 * FB) for c in range(4)]

    def hidden(c):
        both = forward[c].total()
        pre_share[c] = both
        gate, up = both[:, :FB], both[:, FB:]
        hid[forward[c].mine(x), :] = (gate * jax.nn.sigmoid(gate) * up).astype(BF16)
        forward[c].out_send()

    def acts(c):
        grad = backward[c].total()
        gate, up = pre_share[c, :, 0:FB], pre_share[c, :, FB : 2 * FB]
        s = jax.nn.sigmoid(gate)
        mine = backward[c].mine(x)
        act[mine, 0:FB] = (grad * up * s * (1.0 + gate * (1.0 - s))).astype(BF16)
        act[mine, FB : 2 * FB] = (grad * gate * s).astype(BF16)
        backward[c].out_send()

    class ColSum:
        def __init__(self, half, which, part, out):
            self.half, self.part, self.out, self.near = half, part, out, []
            self.c1, self.c2, self.c3 = c1.at[which], c2.at[which], c3.at[which]

        def part_of(self, c, i):
            return rows(c * CHUNK + self.half * PLANE + i * 96, 96)

        def near_send(self, c, i, way):
            to = 0 if way == 1 else 1
            self.near.append(
                transfer(
                    self.part.at[self.part_of(c, i), :],
                    self.c2.at[to, i * 96 : i * 96 + 96, :],
                    along(self.half, major=way),
                )
            )

        def send_far(self):
            self.far = [
                transfer(self.part.at[self.part_of(0, i), :], self.c1.at[i], along(self.half, major=1 - 2 * i))
                for i in (0, 1)
            ]

        def send_near(self, i):
            self.far[i].wait_recv()
            mine = self.part_of(1, i)
            self.part[mine, :] = (self.part[mine, :].astype(F32) + self.c1[i].astype(F32)).astype(BF16)
            self.near_send(1, i, 1 - 2 * i)

        def send_rest(self):
            self.near_send(2, 0, -1)
            self.near_send(2, 1, 1)

        def send_minor(self):
            for copy in self.near:
                copy.wait_recv()
            start = 3 * CHUNK + self.half * PLANE
            own = rows(start, PLANE)
            self.part[own, :] = (
                self.part[own, :].astype(F32) + self.c2[0].astype(F32) + self.c2[1].astype(F32)
            ).astype(BF16)
            self.minor = [
                transfer(
                    self.part.at[rows(start + m * HALF, HALF), :],
                    self.c3.at[m - 1],
                    along(self.half, minor=MINOR_OFF[m]),
                )
                for m in (1, 2, 3)
            ]

        def store(self):
            total = self.part[rows(3 * CHUNK + self.half * PLANE, HALF), :].astype(F32)
            for i in range(3):
                self.minor[i].wait_recv()
                total = total + self.c3[i].astype(F32)
            self.out[rows(self.half * HALF, HALF), :] = total.astype(BF16)

    mixed_sum = [ColSum(h, h, part_m, mixed) for h in (0, 1)]
    ginp_sum = [ColSum(h, 2 + h, part_i, ginp) for h in (0, 1)]

    stores = []

    def tile(i):
        return rows(pl.multiple_of(i * 256, 256), 256)

    def keep(which, i, src, dst):
        copy = pltpu.make_async_copy(src, dst, local.at[16 + which * 4 + i])
        copy.start()
        return copy

    def down_grad(first):
        part = rows(first * CHUNK, 2 * CHUNK)
        gather_g.need(first, first + 1)
        for c in (first, first + 1):
            forward[c].out_wait()

        def body(i, carry):
            new = lax.dot_general(hid[part, :], grads[part, tile(i)], NT, preferred_element_type=F32)
            totals_d[i] = totals_d[i] + new if first else new
            if first:
                keep(2, i, totals_d.at[i], gdown.at[:, tile(i)])
            return carry

        lax.fori_loop(0, 4, body, 0)
        if first:
            for i in range(4):
                stores.append((2, i, totals_d.at[i], gdown.at[:, rows(i * 256, 256)]))

    def up_grad(which, first):
        part, wide = rows(first * CHUNK, 2 * CHUNK), rows(which * FB, FB)
        target = (ggate, gup)[which]
        for c in (first, first + 1):
            backward[c].out_wait()

        def body(i, carry):
            new = lax.dot_general(xs[part, tile(i)], act[part, wide], NT, preferred_element_type=F32)
            totals_u[tile(i), wide] = totals_u[tile(i), wide] + new if first else new
            if first:
                keep(which, i, totals_u.at[tile(i), wide], target.at[tile(i), :])
            return carry

        lax.fori_loop(0, 4, body, 0)
        if first:
            for i in range(4):
                cols = rows(i * 256, 256)
                stores.append((which, i, totals_u.at[cols, wide], target.at[cols, :]))

    gather_x.begin()
    send_tiles()
    gather_x.spread_on(0, 2)
    gather_x.spread_on(0, 1)
    gather_x.forward(0, 0)
    gather_x.spread_on(1, 1)
    gather_x.spread_on(0, 3)
    gather_x.spread_on(1, 2)
    gather_x.forward(1, 0)
    gather_x.spread_on(1, 3)
    tables()
    gather_x.forward(1, 1)
    gather_x.forward(0, 2)
    gather_x.forward(0, 1)
    gather_x.forward(1, 2)
    gather_x.forward(0, 3)
    gather_x.forward(1, 3)
    gather_g.begin()
    permute_most(1)
    permute_most(0)
    permute_rest(0)
    pre_matmul(0, 1)
    gather_g.spread_on(0, 1)
    gather_g.forward(0, 0)
    pre_matmul(0, 0)
    gather_g.spread_on(1, 1)
    forward[0].pair_add(1)
    gather_g.spread_on(0, 3)
    gather_g.spread_on(0, 2)
    gather_g.spread_on(1, 2)
    permute_rest(1)
    forward[0].pair_add(0)
    gather_g.spread_on(1, 3)
    pre_matmul(1, 0)
    gh_matmul(3)
    forward[0].ring_add(1)
    gather_g.forward(1, 1)
    gather_g.forward(0, 1)
    forward[1].pair_add(0)
    gather_g.forward(1, 0)
    pre_matmul(1, 1)
    forward[0].ring_add(0)
    gather_g.forward(0, 3)
    gather_g.forward(1, 2)
    backward[3].pair_add(0)
    permute_most(2)
    gather_g.forward(1, 3)
    forward[1].pair_add(1)
    forward[1].ring_add(0)
    gh_matmul(2)
    permute_rest(2)
    backward[3].ring_add(1)
    gh_matmul(1)
    gather_g.forward(0, 2)
    hidden(0)
    forward[1].ring_add(1)
    backward[2].pair_add(0)
    backward[3].ring_add(0)
    permute_most(3)
    backward[1].pair_add(0)
    permute_rest(3)
    forward[0].out_forward(1)
    gh_matmul(0)
    backward[2].ring_add(0)
    forward[0].out_forward(0)
    hidden(1)
    backward[2].ring_add(1)
    backward[0].pair_add(0)
    backward[1].ring_add(1)
    backward[1].ring_add(0)
    forward[1].out_forward(1)
    forward[0].out_pair()
    mixed_matmul(0)
    forward[1].out_forward(0)
    mixed_sum[1].send_far()
    backward[0].ring_add(1)
    backward[0].ring_add(0)
    pre_matmul(2, 1)
    pre_matmul(2, 0)
    acts(1)
    mixed_sum[0].send_far()
    forward[2].pair_add(1)
    forward[1].out_pair()
    forward[2].pair_add(0)
    down_grad(0)
    acts(0)
    mixed_matmul(1)
    mixed_sum[1].send_near(0)
    mixed_sum[1].send_near(1)
    backward[1].out_forward(1)
    backward[1].out_forward(0)
    mixed_sum[0].send_near(1)
    mixed_sum[0].send_near(0)
    forward[2].ring_add(1)
    forward[2].ring_add(0)
    backward[0].out_forward(1)
    backward[0].out_forward(0)
    pre_matmul(3, 1)
    pre_matmul(3, 0)
    backward[1].out_pair()
    forward[3].pair_add(1)
    forward[3].pair_add(0)
    ginp_matmul(1)
    hidden(2)
    acts(2)
    backward[0].out_pair()
    ginp_matmul(0)
    forward[3].ring_add(1)
    ginp_sum[1].send_far()
    forward[3].ring_add(0)
    ginp_sum[0].send_far()
    up_grad(0, 0)
    up_grad(1, 0)
    forward[2].out_forward(0)
    forward[2].out_forward(1)
    backward[2].out_forward(1)
    backward[2].out_forward(0)
    ginp_sum[1].send_near(0)
    ginp_sum[1].send_near(1)
    ginp_sum[0].send_near(0)
    ginp_sum[0].send_near(1)
    hidden(3)
    acts(3)
    forward[2].out_pair()
    mixed_matmul(2)
    backward[2].out_pair()
    mixed_sum[0].send_rest()
    mixed_sum[1].send_rest()
    forward[3].out_forward(1)
    forward[3].out_forward(0)
    ginp_matmul(2)
    ginp_sum[0].send_rest()
    ginp_sum[1].send_rest()
    backward[3].out_forward(1)
    backward[3].out_forward(0)
    forward[3].out_pair()
    mixed_matmul(3)
    mixed_sum[1].send_minor()
    mixed_sum[0].send_minor()
    backward[3].out_pair()
    down_grad(2)
    ginp_matmul(3)
    ginp_sum[1].send_minor()
    ginp_sum[0].send_minor()
    up_grad(1, 2)
    mixed_sum[1].store()
    up_grad(0, 2)
    mixed_sum[0].store()
    ginp_sum[1].store()
    ginp_sum[0].store()
    for which, i, src, dst in stores:
        pltpu.make_async_copy(src, dst, local.at[16 + which * 4 + i]).wait()
    for copy in sent:
        if id(copy) not in gone:
            copy.wait_send()


STEPS = 4


def hand_over(*refs):
    for src, dst in zip(refs[:5], refs[5:]):
        dst[...] = src[...]


def per_device(loaded, positions, gate_weight, up_weight, down_weight, segment, log_ratio, token_grad):
    vmem, anywhere = pl.BlockSpec(memory_space=pltpu.VMEM), pl.BlockSpec(memory_space=pl.ANY)
    shape = jax.ShapeDtypeStruct
    buf = lambda *s: pltpu.VMEM(s, BF16)
    transfers = 220
    scratch = [
        pltpu.VMEM((128, 128), F32),
        buf(DB, 2 * FB),
        buf(FB, DB),
        buf(TOK, DB),
        buf(TOK, DB),
        buf(TOK, DB),
        buf(TOK, 2 * FB),
        buf(4, PLANE, 2 * FB),
        buf(4, SHARE, 2 * FB),
        buf(4, 2, SHARE, 2 * FB),
        pltpu.VMEM((4, SHARE, 2 * FB), F32),
        buf(TOK, FB),
        buf(TOK, FB),
        buf(4, PLANE, FB),
        buf(4, SHARE, FB),
        buf(4, 2, SHARE, FB),
        buf(TOK, 2 * FB),
        buf(TOK, DB),
        buf(4, 2, 96, DB),
        buf(4, 2, PLANE, DB),
        buf(4, 3, HALF, DB),
        buf(TOK - FAR, CHUNK),
        buf(FAR, CHUNK),
        pltpu.VMEM((TOK, 128), jnp.int32),
        pltpu.VMEM((DB, 2 * FB), F32),
        pltpu.VMEM((4, FB, 256), F32),
        pltpu.VMEM((1, BLOCK), jnp.int32),
        pltpu.VMEM((1, BLOCK), jnp.int32),
        pltpu.VMEM((1, BLOCK), F32),
        buf(BLOCK, DB),
        pltpu.SemaphoreType.DMA((transfers,)),
        pltpu.SemaphoreType.DMA((transfers,)),
        pltpu.SemaphoreType.DMA((32,)),
    ]
    outs = pl.pallas_call(
        kernel,
        out_shape=(
            shape((BLOCK, DB), BF16),
            shape((BLOCK, DB), BF16),
            shape((DB, FB), F32),
            shape((DB, FB), F32),
            shape((FB, DB), F32),
        ),
        in_specs=[anywhere] * 8,
        out_specs=[vmem] * 2 + [anywhere] * 3,
        scratch_shapes=scratch,
        compiler_params=pltpu.CompilerParams(
            collective_id=0, has_side_effects=True, vmem_limit_bytes=64 * 1024 * 1024
        ),
        name="feed_forward",
    )(
        positions.reshape(1, BLOCK), segment.reshape(1, BLOCK), log_ratio.reshape(1, BLOCK),
        loaded, token_grad, gate_weight, up_weight, down_weight,
    )
    blocks = [pl.BlockSpec((BLOCK // 2, DB), lambda i: (jnp.minimum(i, 1), 0))] * 2
    blocks += [pl.BlockSpec((o.shape[0] // STEPS, o.shape[1]), lambda i: (i, 0)) for o in outs[2:]]
    return pl.pallas_call(
        hand_over,
        grid=(STEPS,),
        out_shape=tuple(shape(o.shape, o.dtype) for o in outs),
        in_specs=blocks,
        out_specs=blocks,
        compiler_params=pltpu.CompilerParams(vmem_limit_bytes=64 * 1024 * 1024),
        name="hand_over",
    )(*outs)


def solution(mesh):
    return jax.shard_map(
        per_device,
        mesh=mesh,
        in_specs=(
            P("col", "row"),
            P("col"),
            P("row", "col"),
            P("row", "col"),
            P("col", "row"),
            P("col"),
            P("col"),
            P("col", "row"),
        ),
        out_specs=(
            P("col", "row"),
            P("col", "row"),
            P("row", "col"),
            P("row", "col"),
            P("col", "row"),
        ),
        check_vma=False,
    )
```

```python
import jax
import jax.numpy as jnp
from jax import lax
from jax.experimental import pallas as pl
from jax.experimental.pallas import tpu as pltpu
from jax.sharding import PartitionSpec as P

BETA = 0.1
F32, BF16 = jnp.float32, jnp.bfloat16
TOK, DB, FB = 1536, 1024, 896
BLOCK, HALF = 96, 48
CHUNK, SHARE = 384, 48
PLANE = 192
FAR = 384
PLANE_OFF = (2, 1, -1, 0)
MINOR_OFF = (0, 1, -1, 2)
CHUNKS = (
    ((0, 0), (0, 1), (0, 2), (0, 3)),
    ((1, 0), (1, 1), (2, 2), (2, 3)),
    ((2, 0), (2, 1), (1, 2), (1, 3)),
    ((3, 0), (3, 1), (3, 2), (3, 3)),
)
NT = (((0,), (0,)), ((), ()))
TN = (((1,), (1,)), ((), ()))


def rows(start, size):
    return pl.ds(start, size)


def kernel(spots, parts, ratios, loaded, token_grad, gw, uw, dw, mixed, ginp, ggate, gup, gdown, *scratch):
    (tiles, weights, down, xl, xs, grads, pre, pre_pair, pre_r1, pre_r2, pre_share, hid, ghp, gh_pair,
     gh_r1, gh_r2, act, part_m, c1, c2, c3, onehot, onehot_far, places, totals_u, totals_d, small_u, small_s, small_f, held_grad, send, recv, local) = scratch
    part_i = xl
    row, col = lax.axis_index("row"), lax.axis_index("col")
    x, k, z, y = row // 2, row % 2, col // 4, col % 4

    def device(dx=0, dk=0, dz=0, dy=0):
        return {
            "row": lax.rem(x + dx + 4, 4) * 2 + lax.rem(k + dk, 2),
            "col": lax.rem(z + dz + 4, 4) * 4 + lax.rem(y + dy + 4, 4),
        }

    sent, gone = [], set()

    def transfer(src, dst, target, landing=None):
        index = len(sent)
        copy = pltpu.make_async_remote_copy(
            src_ref=src, dst_ref=dst, send_sem=send.at[index], recv_sem=recv.at[index],
            device_id=target, device_id_type=pl.DeviceIdType.MESH,
        )
        copy.start()
        sent.append(copy)
        if landing is None:
            return copy
        return pltpu.make_async_remote_copy(
            src_ref=src, dst_ref=landing, send_sem=send.at[index], recv_sem=recv.at[index],
            device_id=target, device_id_type=pl.DeviceIdType.MESH,
        )

    local_copies = []

    def fetch(src, dst):
        copy = pltpu.make_async_copy(src, dst, local.at[len(local_copies)])
        copy.start()
        local_copies.append(copy)
        return copy

    def along(half, major=0, minor=0):
        return device(dz=major, dy=minor) if half == 0 else device(dz=minor, dy=major)

    def place(half, plane, minor):
        for c, held in enumerate(CHUNKS):
            if (plane, minor) in held:
                return rows(c * CHUNK + half * PLANE + held.index((plane, minor)) * HALF, HALF)

    sources = (spots, parts, ratios, token_grad)
    spots, parts, ratios, token_grad = small_u, small_s, small_f, held_grad
    first_copies = [
        fetch(loaded.at[rows(half * HALF, HALF), :], xl.at[place(half, 3, 0), :]) for half in (0, 1)
    ]
    small_copies = [fetch(a, b) for a, b in zip(sources, (spots, parts, ratios, token_grad))]
    weight_copies = [fetch(gw, weights.at[:, 0:FB]), fetch(uw, weights.at[:, FB : 2 * FB]), fetch(dw, down)]

    others = [(dz, dy) for dz in range(4) for dy in range(4) if (dz, dy) != (0, 0)]
    barrier = pltpu.get_barrier_semaphore()
    peers = [device(dz=dz, dy=dy) for dz, dy in others]
    peers += [device(dx=1), device(dx=-1), device(dk=1)]
    for peer in peers:
        pl.semaphore_signal(barrier, inc=1, device_id=peer, device_id_type=pl.DeviceIdType.MESH)
    pl.semaphore_wait(barrier, len(peers))

    class Gather:
        def __init__(self, buf):
            self.buf, self.got, self.seen, self.left = buf, {}, set(), False

        def move(self, half, src, dst, target):
            self.got[(half,) + dst] = transfer(
                self.buf.at[place(half, *src)], self.buf.at[place(half, *dst)], target
            )

        def spread(self, half, minor):
            self.move(half, (3, minor), (2, minor), along(half, major=1))
            self.move(half, (3, minor), (1, minor), along(half, major=-1))

        def begin(self):
            for half in (0, 1):
                self.move(half, (3, 0), (3, 2), along(half, minor=1))
                self.move(half, (3, 0), (3, 1), along(half, minor=-1))
                self.move(half, (3, 0), (3, 3), along(half, minor=2))
                self.spread(half, 0)

        def wait(self, half, plane, minor):
            if (half, plane, minor) not in self.seen:
                self.got[(half, plane, minor)].wait_recv()
                self.seen.add((half, plane, minor))

        def spread_on(self, half, minor):
            self.wait(half, 3, minor)
            self.spread(half, minor)

        def forward(self, half, minor):
            plane, way = (2, 1) if minor < 2 else (1, -1)
            self.wait(half, plane, minor)
            self.move(half, (plane, minor), (0, minor), along(half, major=way))

        def need(self, *chunks):
            for c in chunks:
                for half in (0, 1):
                    for plane, minor in CHUNKS[c]:
                        if (plane, minor) != (3, 0):
                            self.wait(half, plane, minor)

    gather_x, gather_g = Gather(xl), Gather(grads)
    for copy in first_copies:
        copy.wait()
    tile_copies = []

    def send_tiles():
        for copy in small_copies:
            copy.wait()
        tiles[0:8, :] = jnp.full((8, 128), -1.0, F32)
        tiles[0:1, 0:BLOCK] = spots[...].astype(F32)
        tiles[1:2, 0:BLOCK] = parts[...].astype(F32)
        tiles[2:3, 0:BLOCK] = ratios[...]
        for dz, dy in others:
            slot = ((-dz) % 4) * 4 + (-dy) % 4
            tile_copies.append(
                transfer(tiles.at[0:8, :], tiles.at[slot * 8 : slot * 8 + 8, :], device(dz=dz, dy=dy))
            )

    def slot_of(half, plane, minor):
        major, less = PLANE_OFF[plane] % 4, MINOR_OFF[minor] % 4
        return major * 4 + less if half == 0 else less * 4 + major

    def tables():
        for copy in tile_copies:
            copy.wait_recv()
        table = tiles[...]
        turned = table.T
        for half in (0, 1):
            for plane in range(4):
                for minor in range(4):
                    lane = slot_of(half, plane, minor) * 8
                    column = turned[half * HALF : half * HALF + HALF, lane : lane + 1]
                    places[place(half, plane, minor), :] = jnp.broadcast_to(column, (HALF, 128)).astype(jnp.int32)
        segment_part = jnp.concatenate([table[8 * i + 1 : 8 * i + 2, :] for i in range(16)], 0)
        ratio_part = jnp.concatenate([table[8 * i + 2 : 8 * i + 3, :] for i in range(16)], 0)

        def total(s):
            return jnp.sum(jnp.where(segment_part == float(s), ratio_part, 0.0), axis=(0, 1), keepdims=True)

        own_segment = turned[0:BLOCK, 1:2]
        token_weight = jnp.zeros((BLOCK, 1), F32)
        for p in range(4):
            margin = BETA * (total(2 * p) - total(2 * p + 1))
            pair_weight = -BETA * jax.nn.sigmoid(-margin)
            token_weight = jnp.where(own_segment == float(2 * p), pair_weight, token_weight)
            token_weight = jnp.where(own_segment == float(2 * p + 1), -pair_weight, token_weight)
        for half in (0, 1):
            part = rows(half * HALF, HALF)
            weight = token_weight[half * HALF : half * HALF + HALF, :]
            grads[place(half, 3, 0), :] = (weight * token_grad[part, :].astype(F32)).astype(BF16)

    ready = []

    def need_weights():
        if not ready:
            for copy in weight_copies:
                copy.wait()
            ready.append(True)

    def tokens_of(c):
        lane = lax.broadcasted_iota(jnp.int32, (1, CHUNK), 1)
        token = lane
        for j in range(8):
            half, (plane, minor) = j // 4, CHUNKS[c][j % 4]
            major, less = PLANE_OFF[plane], MINOR_OFF[minor]
            dz, dy = (major, less) if half == 0 else (less, major)
            block = lax.rem(z + dz + 4, 4) * 4 + lax.rem(y + dy + 4, 4)
            inside = (lane >= j * HALF) & (lane < (j + 1) * HALF)
            token = token + jnp.where(inside, block * BLOCK + half * HALF - j * HALF, 0)
        return token

    def match(c, first, count, ref):
        token = tokens_of(c)

        def build(i, carry):
            part = rows(pl.multiple_of(i * 128, 128), 128)
            here = places[rows(pl.multiple_of(first + i * 128, 128), 128), :]
            for j in range(0, CHUNK, 128):
                ref[part, j : j + 128] = jnp.where(here == token[:, j : j + 128], 1.0, 0.0).astype(BF16)
            return carry

        lax.fori_loop(0, count // 128, build, 0)

    def permute_most(c):
        gather_x.need(1, 2, 3)
        match(c, FAR, TOK - FAR, onehot)
        xs[rows(c * CHUNK, CHUNK), :] = lax.dot_general(
            onehot[...], xl[FAR:TOK, :], NT, preferred_element_type=F32
        ).astype(BF16)

    def permute_rest(c):
        gather_x.need(0)
        match(c, 0, FAR, onehot_far)
        chunk = rows(c * CHUNK, CHUNK)
        rest = lax.dot_general(onehot_far[...], xl[0:FAR, :], NT, preferred_element_type=F32)
        xs[chunk, :] = (xs[chunk, :].astype(F32) + rest).astype(BF16)

    def pre_matmul(c, i):
        need_weights()
        chunk, cols = rows(c * CHUNK, CHUNK), rows(i * FB, FB)
        pre[chunk, cols] = jnp.dot(xs[chunk, :], weights[:, cols], preferred_element_type=F32).astype(BF16)
        forward[c].pair_send(i)

    def gh_matmul(c):
        need_weights()
        gather_g.need(c)
        chunk = rows(c * CHUNK, CHUNK)
        ghp[chunk, :] = lax.dot_general(grads[chunk, :], down[...], TN, preferred_element_type=F32).astype(BF16)
        backward[c].pair_send(0)

    def mixed_matmul(c):
        chunk = rows(c * CHUNK, CHUNK)
        forward[c].out_wait()
        part_m[chunk, :] = jnp.dot(hid[chunk, :], down[...], preferred_element_type=F32).astype(BF16)

    def ginp_matmul(c):
        chunk = rows(c * CHUNK, CHUNK)
        backward[c].out_wait()
        if not gather_x.left:
            gather_x.left = True
            for copy in gather_x.got.values():
                copy.wait_send()
                gone.add(id(copy))
        part_i[chunk, :] = lax.dot_general(
            act[chunk, :], weights[...], TN, preferred_element_type=F32
        ).astype(BF16)

    xp, xm, xo = lax.rem(x + 1, 4), lax.rem(x + 3, 4), lax.rem(x + 2, 4)

    class RowChunk:
        def __init__(self, c, part, pair, r1, r2, width, out, out_width):
            self.c, self.part, self.pair, self.r1, self.r2 = c, part, pair, r1, r2
            self.width, self.out, self.out_width = width, out, out_width
            self.pairs, self.far, self.near, self.last = {}, {}, {}, {}

        def cut(self, width):
            if width == 2 * FB:
                return FB
            return 512 if self.c % 2 == 0 else 384

        def mine(self, xx):
            return rows(pl.multiple_of(self.c * CHUNK + k * PLANE + xx * SHARE, 16), SHARE)

        def pair_send(self, i):
            theirs = rows(pl.multiple_of(self.c * CHUNK + (1 - k) * PLANE, 16), PLANE)
            cols = rows(i * FB, FB)
            self.pairs[i] = transfer(self.part.at[theirs, cols], self.pair.at[self.c, :, cols], device(dk=1))

        def pair_add(self, i):
            self.pairs[i].wait_recv()
            mine, cols = rows(pl.multiple_of(self.c * CHUNK + k * PLANE, 16), PLANE), rows(i * FB, FB)
            both = self.part[mine, cols].astype(F32) + self.pair[self.c, :, cols].astype(F32)
            self.part[mine, cols] = both.astype(BF16)
            cut, far = self.cut(self.width), self.mine(xo)
            for way, lo, hi, dx in ((0, 0, cut, 1), (1, cut, self.width, -1)):
                if self.width == FB or way == i:
                    self.far[way] = transfer(
                        self.part.at[far, lo:hi], self.r1.at[self.c, :, lo:hi], device(dx=dx)
                    )

        def ring_add(self, i):
            cut = self.cut(self.width)
            xx, lo, hi, dx = ((xp, 0, cut, 1), (xm, cut, self.width, -1))[i]
            self.far[i].wait_recv()
            mine = self.mine(xx)
            both = self.part[mine, lo:hi].astype(F32) + self.r1[self.c, :, lo:hi].astype(F32)
            self.part[mine, lo:hi] = both.astype(BF16)
            self.near[i] = transfer(self.part.at[mine, :], self.r2.at[self.c, i], device(dx=dx))

        def total(self):
            self.near[0].wait_recv()
            self.near[1].wait_recv()
            return (
                self.part[self.mine(x), :].astype(F32)
                + self.r2[self.c, 0].astype(F32)
                + self.r2[self.c, 1].astype(F32)
            )

        def out_send(self):
            own = self.out.at[self.mine(x), :]
            self.side = [
                transfer(own, own, device(dx=1), self.out.at[self.mine(xm), :]),
                transfer(own, own, device(dx=-1), self.out.at[self.mine(xp), :]),
            ]
            self.done = []
            self.over(x)

        def over(self, xx):
            mine = self.out.at[self.mine(xx), :]
            other = rows(pl.multiple_of(self.c * CHUNK + (1 - k) * PLANE + xx * SHARE, 16), SHARE)
            self.done.append(transfer(mine, mine, device(dk=1), self.out.at[other, :]))

        def out_forward(self, i):
            cut = self.cut(self.out_width)
            xx, lo, hi, dx = ((xm, 0, cut, 1), (xp, cut, self.out_width, -1))[i]
            self.side[i].wait_recv()
            piece = self.out.at[self.mine(xx), lo:hi]
            self.last[i] = transfer(piece, piece, device(dx=dx), self.out.at[self.mine(xo), lo:hi])
            self.over(xx)

        def out_pair(self):
            self.last[0].wait_recv()
            self.last[1].wait_recv()
            self.over(xo)

        def out_wait(self):
            for copy in self.done:
                copy.wait_recv()
            self.done = []

    forward = [RowChunk(c, pre, pre_pair, pre_r1, pre_r2, 2 * FB, hid, FB) for c in range(4)]
    backward = [RowChunk(c, ghp, gh_pair, gh_r1, gh_r2, FB, act, 2 * FB) for c in range(4)]

    def hidden(c):
        both = forward[c].total()
        pre_share[c] = both
        gate, up = both[:, :FB], both[:, FB:]
        hid[forward[c].mine(x), :] = (gate * jax.nn.sigmoid(gate) * up).astype(BF16)
        forward[c].out_send()

    def acts(c):
        grad = backward[c].total()
        gate, up = pre_share[c, :, 0:FB], pre_share[c, :, FB : 2 * FB]
        s = jax.nn.sigmoid(gate)
        mine = backward[c].mine(x)
        act[mine, 0:FB] = (grad * up * s * (1.0 + gate * (1.0 - s))).astype(BF16)
        act[mine, FB : 2 * FB] = (grad * gate * s).astype(BF16)
        backward[c].out_send()

    class ColSum:
        def __init__(self, half, which, part, out):
            self.half, self.part, self.out, self.near = half, part, out, []
            self.c1, self.c2, self.c3 = c1.at[which], c2.at[which], c3.at[which]

        def part_of(self, c, i):
            return rows(c * CHUNK + self.half * PLANE + i * 96, 96)

        def near_send(self, c, i, way):
            to = 0 if way == 1 else 1
            self.near.append(
                transfer(
                    self.part.at[self.part_of(c, i), :],
                    self.c2.at[to, i * 96 : i * 96 + 96, :],
                    along(self.half, major=way),
                )
            )

        def send_far(self):
            self.far = [
                transfer(self.part.at[self.part_of(0, i), :], self.c1.at[i], along(self.half, major=1 - 2 * i))
                for i in (0, 1)
            ]

        def send_near(self, i):
            self.far[i].wait_recv()
            mine = self.part_of(1, i)
            self.part[mine, :] = (self.part[mine, :].astype(F32) + self.c1[i].astype(F32)).astype(BF16)
            self.near_send(1, i, 1 - 2 * i)

        def send_rest(self):
            self.near_send(2, 0, -1)
            self.near_send(2, 1, 1)

        def send_minor(self):
            for copy in self.near:
                copy.wait_recv()
            start = 3 * CHUNK + self.half * PLANE
            own = rows(start, PLANE)
            self.part[own, :] = (
                self.part[own, :].astype(F32) + self.c2[0].astype(F32) + self.c2[1].astype(F32)
            ).astype(BF16)
            self.minor = [
                transfer(
                    self.part.at[rows(start + m * HALF, HALF), :],
                    self.c3.at[m - 1],
                    along(self.half, minor=MINOR_OFF[m]),
                )
                for m in (1, 2, 3)
            ]

        def store(self):
            total = self.part[rows(3 * CHUNK + self.half * PLANE, HALF), :].astype(F32)
            for i in range(3):
                self.minor[i].wait_recv()
                total = total + self.c3[i].astype(F32)
            self.out[rows(self.half * HALF, HALF), :] = total.astype(BF16)

    mixed_sum = [ColSum(h, h, part_m, mixed) for h in (0, 1)]
    ginp_sum = [ColSum(h, 2 + h, part_i, ginp) for h in (0, 1)]

    stores = []

    def tile(i):
        return rows(pl.multiple_of(i * 256, 256), 256)

    def keep(which, i, src, dst):
        copy = pltpu.make_async_copy(src, dst, local.at[16 + which * 4 + i])
        copy.start()
        return copy

    def down_grad(first):
        part = rows(first * CHUNK, 2 * CHUNK)
        gather_g.need(first, first + 1)
        for c in (first, first + 1):
            forward[c].out_wait()

        def body(i, carry):
            new = lax.dot_general(hid[part, :], grads[part, tile(i)], NT, preferred_element_type=F32)
            totals_d[i] = totals_d[i] + new if first else new
            if first:
                keep(2, i, totals_d.at[i], gdown.at[:, tile(i)])
            return carry

        lax.fori_loop(0, 4, body, 0)
        if first:
            for i in range(4):
                stores.append((2, i, totals_d.at[i], gdown.at[:, rows(i * 256, 256)]))

    def up_grad(which, first):
        part, wide = rows(first * CHUNK, 2 * CHUNK), rows(which * FB, FB)
        target = (ggate, gup)[which]
        for c in (first, first + 1):
            backward[c].out_wait()

        def body(i, carry):
            new = lax.dot_general(xs[part, tile(i)], act[part, wide], NT, preferred_element_type=F32)
            totals_u[tile(i), wide] = totals_u[tile(i), wide] + new if first else new
            if first:
                keep(which, i, totals_u.at[tile(i), wide], target.at[tile(i), :])
            return carry

        lax.fori_loop(0, 4, body, 0)
        if first:
            for i in range(4):
                cols = rows(i * 256, 256)
                stores.append((which, i, totals_u.at[cols, wide], target.at[cols, :]))

    gather_x.begin()
    gather_x.spread_on(1, 2)
    gather_x.spread_on(0, 1)
    send_tiles()
    gather_x.spread_on(0, 3)
    gather_x.spread_on(1, 3)
    gather_x.spread_on(1, 1)
    gather_x.spread_on(0, 2)
    tables()
    gather_x.forward(0, 0)
    gather_x.forward(1, 0)
    gather_x.forward(0, 1)
    gather_x.forward(1, 2)
    gather_x.forward(1, 3)
    gather_x.forward(0, 3)
    gather_x.forward(1, 1)
    gather_x.forward(0, 2)
    gather_g.begin()
    permute_most(0)
    permute_most(2)
    permute_rest(0)
    pre_matmul(0, 1)
    pre_matmul(0, 0)
    permute_rest(2)
    forward[0].pair_add(1)
    pre_matmul(2, 0)
    forward[0].pair_add(0)
    pre_matmul(2, 1)
    gather_g.spread_on(1, 3)
    forward[2].pair_add(0)
    gather_g.spread_on(0, 2)
    forward[2].pair_add(1)
    gather_g.spread_on(1, 2)
    gather_g.spread_on(0, 3)
    forward[0].ring_add(0)
    forward[0].ring_add(1)
    gh_matmul(3)
    permute_most(1)
    gather_g.spread_on(0, 1)
    gather_g.forward(1, 3)
    forward[2].ring_add(0)
    permute_rest(1)
    forward[2].ring_add(1)
    gather_g.forward(0, 3)
    gather_g.spread_on(1, 1)
    pre_matmul(1, 0)
    pre_matmul(1, 1)
    hidden(0)
    gather_g.forward(0, 1)
    gather_g.forward(0, 2)
    gather_g.forward(1, 2)
    forward[1].pair_add(1)
    gather_g.forward(1, 1)
    forward[1].pair_add(0)
    gather_g.forward(0, 0)
    gather_g.forward(1, 0)
    hidden(2)
    forward[0].out_forward(0)
    gh_matmul(1)
    forward[0].out_forward(1)
    backward[1].pair_add(0)
    forward[1].ring_add(1)
    forward[1].ring_add(0)
    gh_matmul(0)
    permute_most(3)
    backward[0].pair_add(0)
    forward[2].out_forward(0)
    backward[1].ring_add(0)
    forward[0].out_pair()
    backward[1].ring_add(1)
    forward[2].out_forward(1)
    mixed_matmul(0)
    backward[0].ring_add(1)
    hidden(1)
    backward[0].ring_add(0)
    forward[2].out_pair()
    acts(1)
    mixed_matmul(2)
    forward[1].out_forward(0)
    permute_rest(3)
    pre_matmul(3, 0)
    acts(0)
    pre_matmul(3, 1)
    mixed_sum[1].send_far()
    gh_matmul(2)
    backward[1].out_forward(0)
    forward[1].out_forward(1)
    backward[2].pair_add(0)
    forward[3].pair_add(1)
    backward[0].out_forward(1)
    backward[1].out_forward(1)
    mixed_sum[0].send_far()
    backward[0].out_forward(0)
    backward[3].pair_add(0)
    forward[1].out_pair()
    mixed_matmul(1)
    backward[2].ring_add(1)
    forward[3].pair_add(0)
    backward[2].ring_add(0)
    mixed_sum[0].send_rest()
    mixed_sum[1].send_near(0)
    forward[3].ring_add(1)
    mixed_sum[0].send_near(1)
    backward[0].out_pair()
    backward[1].out_pair()
    mixed_sum[1].send_near(1)
    forward[3].ring_add(0)
    ginp_matmul(0)
    ginp_sum[0].send_far()
    acts(2)
    ginp_sum[1].send_far()
    ginp_matmul(1)
    down_grad(0)
    mixed_sum[0].send_near(0)
    hidden(3)
    up_grad(0, 0)
    backward[3].ring_add(1)
    backward[3].ring_add(0)
    mixed_sum[1].send_rest()
    ginp_sum[1].send_near(1)
    ginp_sum[0].send_near(0)
    backward[2].out_forward(0)
    backward[2].out_forward(1)
    up_grad(1, 0)
    forward[3].out_forward(0)
    forward[3].out_forward(1)
    acts(3)
    ginp_sum[0].send_near(1)
    ginp_sum[1].send_near(0)
    backward[2].out_pair()
    forward[3].out_pair()
    ginp_matmul(2)
    ginp_sum[1].send_rest()
    ginp_sum[0].send_rest()
    mixed_matmul(3)
    backward[3].out_forward(0)
    backward[3].out_forward(1)
    down_grad(2)
    mixed_sum[0].send_minor()
    mixed_sum[1].send_minor()
    backward[3].out_pair()
    ginp_matmul(3)
    ginp_sum[0].send_minor()
    ginp_sum[1].send_minor()
    up_grad(0, 2)
    up_grad(1, 2)
    mixed_sum[1].store()
    mixed_sum[0].store()
    ginp_sum[0].store()
    ginp_sum[1].store()
    for which, i, src, dst in stores:
        pltpu.make_async_copy(src, dst, local.at[16 + which * 4 + i]).wait()
    for copy in sent:
        if id(copy) not in gone:
            copy.wait_send()


STEPS = 4


def hand_over(*refs):
    for src, dst in zip(refs[:5], refs[5:]):
        dst[...] = src[...]


def per_device(loaded, positions, gate_weight, up_weight, down_weight, segment, log_ratio, token_grad):
    vmem, anywhere = pl.BlockSpec(memory_space=pltpu.VMEM), pl.BlockSpec(memory_space=pl.ANY)
    shape = jax.ShapeDtypeStruct
    buf = lambda *s: pltpu.VMEM(s, BF16)
    transfers = 220
    scratch = [
        pltpu.VMEM((128, 128), F32),
        buf(DB, 2 * FB),
        buf(FB, DB),
        buf(TOK, DB),
        buf(TOK, DB),
        buf(TOK, DB),
        buf(TOK, 2 * FB),
        buf(4, PLANE, 2 * FB),
        buf(4, SHARE, 2 * FB),
        buf(4, 2, SHARE, 2 * FB),
        pltpu.VMEM((4, SHARE, 2 * FB), F32),
        buf(TOK, FB),
        buf(TOK, FB),
        buf(4, PLANE, FB),
        buf(4, SHARE, FB),
        buf(4, 2, SHARE, FB),
        buf(TOK, 2 * FB),
        buf(TOK, DB),
        buf(4, 2, 96, DB),
        buf(4, 2, PLANE, DB),
        buf(4, 3, HALF, DB),
        buf(TOK - FAR, CHUNK),
        buf(FAR, CHUNK),
        pltpu.VMEM((TOK, 128), jnp.int32),
        pltpu.VMEM((DB, 2 * FB), F32),
        pltpu.VMEM((4, FB, 256), F32),
        pltpu.VMEM((1, BLOCK), jnp.int32),
        pltpu.VMEM((1, BLOCK), jnp.int32),
        pltpu.VMEM((1, BLOCK), F32),
        buf(BLOCK, DB),
        pltpu.SemaphoreType.DMA((transfers,)),
        pltpu.SemaphoreType.DMA((transfers,)),
        pltpu.SemaphoreType.DMA((32,)),
    ]
    outs = pl.pallas_call(
        kernel,
        out_shape=(
            shape((BLOCK, DB), BF16),
            shape((BLOCK, DB), BF16),
            shape((DB, FB), F32),
            shape((DB, FB), F32),
            shape((FB, DB), F32),
        ),
        in_specs=[anywhere] * 8,
        out_specs=[vmem] * 2 + [anywhere] * 3,
        scratch_shapes=scratch,
        compiler_params=pltpu.CompilerParams(
            collective_id=0, has_side_effects=True, vmem_limit_bytes=64 * 1024 * 1024
        ),
        name="feed_forward",
    )(
        positions.reshape(1, BLOCK), segment.reshape(1, BLOCK), log_ratio.reshape(1, BLOCK),
        loaded, token_grad, gate_weight, up_weight, down_weight,
    )
    blocks = [pl.BlockSpec((BLOCK // 2, DB), lambda i: (jnp.minimum(i, 1), 0))] * 2
    blocks += [pl.BlockSpec((o.shape[0] // STEPS, o.shape[1]), lambda i: (i, 0)) for o in outs[2:]]
    return pl.pallas_call(
        hand_over,
        grid=(STEPS,),
        out_shape=tuple(shape(o.shape, o.dtype) for o in outs),
        in_specs=blocks,
        out_specs=blocks,
        compiler_params=pltpu.CompilerParams(vmem_limit_bytes=64 * 1024 * 1024),
        name="hand_over",
    )(*outs)


def solution(mesh):
    return jax.shard_map(
        per_device,
        mesh=mesh,
        in_specs=(
            P("col", "row"),
            P("col"),
            P("row", "col"),
            P("row", "col"),
            P("col", "row"),
            P("col"),
            P("col"),
            P("col", "row"),
        ),
        out_specs=(
            P("col", "row"),
            P("col", "row"),
            P("row", "col"),
            P("row", "col"),
            P("col", "row"),
        ),
        check_vma=False,
    )
```
